128 devices in a mesh: sub: 32 (over z, x, core), grp: 4 (over y).
Axes of the slice: x: 4, y: 4, z: 4, core: 2. Of those that a mesh axis runs over, the one named last changes fastest.
Arguments:
- residual: float32 [32, 128, 4608], P('sub', None, 'grp'), may hold values from -8 to 8
- neumann: bfloat16 [32, 4608, 4608], P('sub', 'grp'), may hold values from -0.09375 to 0.09375
- projection: bfloat16 [32, 4, 4, 768, 1024], P('sub', 'grp'), may hold values from -0.21875 to 0.21875
- pair_list: int32 [32, 4, 4, 2], replicated, may hold values from 0 to 31, as said below
- slave_dofs: int32 [32, 4, 2, 768], P('sub', 'grp'), may hold values from 0 to 1151, as said below
- master_dofs: int32 [32, 4, 4, 1024], P('sub', 'grp'), may hold values from 0 to 1151, as said below
- zbasis: float32 [32, 48, 4608], P('sub'), may hold values from -0.09375 to 0.09375
- ybasis: float32 [32, 48, 4608], P('sub'), may hold values from -0.21875 to 0.21875
- coarse_inverse: float32 [768, 768], replicated, may hold values from -0.21875 to 0.21875
- coarse_ids: int32 [32], P('sub'), may hold values from 0 to 15
Outputs:
- balanced: float32 [32, 128, 4608], P('sub', None, 'grp')
- correction: float32 [32, 128, 4608], P('sub', None, 'grp')
The draws below stay inside these ranges and needn't reach their ends.
Inputs may be any that keep to these rules, and one draw needn't show every extreme that they name: `pair_list`: entry [s, g, j] holds the slave subdomain b of pair j of region g of subdomain s, then the number of b's slave face in region g. b is s + k modulo 32 for some k with 1 <= |k| <= 2; in each region no k is used by more than 2 pairs, and at least one k is used by exactly 2. `slave_dofs`: each face lists distinct positions within its region. `master_dofs`: each face lists distinct positions within its region.
All inputs are finite; a program needn't handle non-finite values.
Results may differ from the reference program's by a relative error of at most 0.0041.
Values may be sent and summed in bfloat16 or wider, within the bound.
A program may use at most 128 MiB of HBM per device.

```python
import jax
import jax.numpy as jnp
from jax import lax

IF = 4608
FS = 768
FM = 1024
NC = 48
COLS = 128
PAIRS = 4
SFACES = 2
RANGE = 2
CAP = 2
CBLK = 16
SUBS = 32
GROUPS = 4
ROWS = 1152


def pick_positions(key, count, width):
    keys = jax.random.split(key, count)
    return jax.vmap(lambda one_key: jax.random.permutation(one_key, IF // GROUPS)[:width])(keys).astype(jnp.int32)


def draw_pair_list(key, part):
    key = jax.random.fold_in(key, 11)
    count = SUBS * GROUPS
    keys = jax.random.split(key, count)
    slots = 2 * RANGE * CAP

    def one_region(one_key):
        key_first, key_order, key_shuffle, key_faces = jax.random.split(one_key, 4)
        first = jax.random.randint(key_first, (), 0, 2 * RANGE)
        order = jax.random.permutation(key_order, slots)
        labels = order // CAP
        score = jnp.where(labels == first, slots, 0) + jnp.arange(slots)
        others = labels[jnp.argsort(score, stable=True)][:PAIRS - CAP]
        chosen = jnp.concatenate([jnp.full((CAP,), first, jnp.int32), others.astype(jnp.int32)])
        chosen = chosen[jax.random.permutation(key_shuffle, PAIRS)]
        faces = jax.random.randint(key_faces, (PAIRS,), 0, SFACES)
        return (chosen, faces)
    labels, faces = jax.vmap(one_region)(keys)
    distance = jnp.where(labels < RANGE, labels - RANGE, labels - RANGE + 1)
    owners = (jnp.arange(count, dtype=jnp.int32) // GROUPS)[:, None]
    slaves = (owners + distance) % SUBS
    return jnp.stack([slaves, faces.astype(jnp.int32)], -1).reshape(SUBS, GROUPS, PAIRS, 2).astype(jnp.int32)


def draw_slave_dofs(key, part):
    key = jax.random.fold_in(key, 12)
    return pick_positions(key, SUBS * GROUPS * SFACES, FS).reshape(SUBS, GROUPS, SFACES, FS)


def draw_master_dofs(key, part):
    key = jax.random.fold_in(key, 13)
    return pick_positions(key, SUBS * GROUPS * PAIRS, FM).reshape(SUBS, GROUPS, PAIRS, FM)


def place_ends(result, own_key, least, largest):
    longest = result.shape.index(max(result.shape))
    spots = []
    for shift in (0, 1):
        where = [jax.random.randint(jax.random.fold_in(own_key, axis), (), 0, length) for axis, length in enumerate(result.shape)]
        where[longest] = (where[longest] + shift) % result.shape[longest]
        spots.append(tuple(where))
    return result.at[spots[0]].set(least).at[spots[1]].set(largest)


def block_scale(key, dims, cuts, least, largest):
    def one(axis_at, parts):
        draws = jax.random.uniform(jax.random.fold_in(jax.random.fold_in(key, 6), axis_at), (parts,), jnp.float32, least / len(cuts), largest / len(cuts))
        return jnp.repeat(jnp.exp(draws), dims[axis_at] // parts).reshape((-1,) + (1,) * (len(dims) - axis_at - 1))

    loudness = one(*cuts[0])
    for cut in cuts[1:]:
        loudness = loudness * one(*cut)
    return loudness


def gaussian(own_key, extent, deviation, reach, cuts=(), kind=jnp.bfloat16):
    drawn = jax.random.normal(own_key, extent, jnp.float32) * deviation
    if len(cuts) > 0:
        drawn = block_scale(own_key, extent, cuts, -0.22, 0.18) * drawn
    return jnp.clip(drawn, min=-reach, max=reach).astype(kind)


def setup_inputs(seed: int = 0) -> dict:
    key_of = jax.random.split(jax.random.key(seed), 11)
    return {
        "residual": gaussian(key_of[0], (SUBS, COLS, IF), 1.0, 8.0, ((0, 32), (2, 4)), jnp.float32),
        "neumann": gaussian(key_of[1], (SUBS, IF, IF), IF ** -0.5, 0.09375, ((0, 32), (1, 4))),
        "projection": gaussian(key_of[2], (SUBS, GROUPS, PAIRS, FS, FM), FS ** -0.5, 0.21875, ((0, 32), (1, 4))),
        "pair_list": draw_pair_list(jax.random.fold_in(key_of[10], 71), 0),
        "slave_dofs": draw_slave_dofs(jax.random.fold_in(key_of[10], 71), 0),
        "master_dofs": draw_master_dofs(jax.random.fold_in(key_of[10], 71), 0),
        "zbasis": gaussian(key_of[6], (SUBS, NC, IF), IF ** -0.5, 0.09375, ((0, 32),), jnp.float32),
        "ybasis": gaussian(key_of[7], (SUBS, NC, IF), (16 * NC) ** -0.5, 0.21875, ((0, 32),), jnp.float32),
        "coarse_inverse": gaussian(key_of[8], (CBLK * NC, CBLK * NC), (CBLK * NC) ** -0.5, 0.21875, (), jnp.float32),
        "coarse_ids": place_ends(jax.random.randint(key_of[9], (SUBS,), 0, CBLK), jax.random.fold_in(key_of[9], 1), 0, CBLK - 1).astype(jnp.int32),
    }


def wide_dot(left_side, right_side, left_dim, right_dim):
    return lax.dot_general(left_side.astype(jnp.float32), right_side.astype(jnp.float32),
                           (((left_dim,), (right_dim,)), ((), ())), precision=lax.Precision.HIGHEST)


def pair_terms(residual, projection, pair_list, slave_dofs, master_dofs):
    regions = residual.reshape(SUBS, COLS, GROUPS, ROWS)

    def one_pair(pair_at):
        owner_sub = pair_at // (GROUPS * PAIRS)
        group_at = (pair_at // PAIRS) % GROUPS
        column = pair_at % PAIRS
        slave_sub = pair_list[owner_sub, group_at, column, 0]
        face_id = pair_list[owner_sub, group_at, column, 1]
        slave_idx = slave_dofs[slave_sub, group_at, face_id]
        master_idx = master_dofs[owner_sub, group_at, column]
        slave_trace = jnp.take(regions[slave_sub, :, group_at, :], slave_idx, axis=1).astype(jnp.bfloat16)
        matrix = projection[owner_sub, group_at, column]
        mismatch = wide_dot(slave_trace, matrix, 1, 0)
        mismatch = mismatch - jnp.take(regions[owner_sub, :, group_at, :], master_idx, axis=1)
        returned = wide_dot(mismatch.astype(jnp.bfloat16), matrix, 1, 1).astype(jnp.bfloat16)
        return mismatch, returned

    return lax.map(one_pair, jnp.arange(SUBS * GROUPS * PAIRS, dtype=jnp.int32))


def reference(residual, neumann, projection, pair_list, slave_dofs, master_dofs, zbasis, ybasis, coarse_inverse, coarse_ids):
    highest = lax.Precision.HIGHEST
    mismatch, returned = pair_terms(residual, projection, pair_list, slave_dofs, master_dofs)
    pair_ids = jnp.arange(SUBS * GROUPS * PAIRS, dtype=jnp.int32)
    owner_sub = pair_ids // (GROUPS * PAIRS)
    group_at = (pair_ids // PAIRS) % GROUPS
    flat_list = pair_list.reshape(SUBS * GROUPS * PAIRS, 2)
    slave_sub = flat_list[:, 0]
    face_id = flat_list[:, 1]
    master_idx = master_dofs.reshape(SUBS * GROUPS * PAIRS, FM)
    slave_idx = slave_dofs[slave_sub, group_at, face_id]
    layout = residual.reshape(SUBS, COLS, GROUPS, ROWS).transpose(0, 2, 3, 1)
    layout = layout.at[owner_sub[:, None], group_at[:, None], master_idx].add(0.5 * mismatch.transpose(0, 2, 1))
    layout = layout.at[slave_sub[:, None], group_at[:, None], slave_idx].add(
        -0.5 * returned.astype(jnp.float32).transpose(0, 2, 1))
    balanced = layout.transpose(0, 3, 1, 2).reshape(SUBS, COLS, IF)
    coarse_part = jnp.einsum('snd,scd->snc', zbasis, balanced, precision=highest)
    selector = (coarse_ids[:, None] == jnp.arange(CBLK, dtype=jnp.int32)[None, :]).astype(jnp.float32)
    coarse_residual = jnp.einsum('sk,snc->knc', selector, coarse_part, precision=highest)
    multipliers = jnp.dot(coarse_inverse, coarse_residual.reshape(CBLK * NC, COLS), precision=highest)
    multipliers = multipliers.reshape(CBLK, NC, COLS)
    chosen = jnp.einsum('sk,knc->snc', selector, multipliers, precision=highest)
    neumann_input = (balanced - jnp.einsum('snc,snd->scd', chosen, ybasis, precision=highest)).astype(jnp.bfloat16)

    def solve_one(operands):
        return wide_dot(operands[0], operands[1], 1, 1)

    neumann_out = lax.map(solve_one, (neumann_input, neumann))
    correction = jnp.einsum('snc,snd->scd', chosen, zbasis, precision=highest) + neumann_out
    return balanced, correction
```

```python
import jax
import jax.numpy as jnp
from jax import lax
from jax.experimental import pallas as pl
from jax.experimental.pallas import tpu as pltpu
from jax.sharding import PartitionSpec as P

FS = 768
FM = 1024
NC = 48
COLS = 128
PAIRS = 4
ROWS = 1152
SUBS = 32
GROUPS = 4
CBLK = 16
REACH = (-2, -1, 1, 2)
HALF = COLS // 2
EXT = FS + 16
F32 = jnp.float32
BF16 = jnp.bfloat16
MESH = pl.DeviceIdType.MESH


def mm_nn(a, b):
    return lax.dot_general(a, b, (((1,), (0,)), ((), ())), preferred_element_type=F32)


def mm_nt(a, b):
    return lax.dot_general(a, b, (((1,), (1,)), ((), ())), preferred_element_type=F32)


def split(x):
    hi = x.astype(BF16)
    return hi, (x - hi.astype(F32)).astype(BF16)


def one_hot(cond):
    return jnp.where(cond, 1.0, 0.0).astype(BF16)


def kernel(
    pair_h, ids_s, res_h, neu_h, proj_h, sdof_h, mdof_h, zb_h, yb_h, cinv_h,
    bal_h, cor_h,
    pair_s, res_v, rbf_v, rin_v, sdof_v, sdin_v, mdof_v, proj_v, u_v, st_v, gt_v,
    neu_v, z_v, y_v, cinv_v, idv_v, idin_v, exp_v, a_v, part_v, m_v, wcat_v, wacc_v,
    base_v, tr_v, mm_v, ret_v, t_v, reply_v, rpin_v, gath_v, acc_v,
    loc_sem, sd_send, sd_recv, rs_send, rs_recv, rp_send, rp_recv,
    id_send, id_recv, pt_send, pt_recv, g_send, g_recv, m_send, m_recv,
):
    s = lax.axis_index("sub")
    g = lax.axis_index("grp")

    def sub_dev(step):
        return (lax.rem(s + step + SUBS, SUBS), g)

    def grp_dev(step):
        return (s, lax.rem(g + step, GROUPS))

    barrier = pltpu.get_barrier_semaphore()

    def greet(r, c):
        pl.semaphore_signal(barrier, inc=1, device_id=sub_dev(r), device_id_type=MESH)
        return c

    lax.fori_loop(1, SUBS, greet, 0)
    for r in range(1, GROUPS):
        pl.semaphore_signal(barrier, inc=1, device_id=grp_dev(r), device_id_type=MESH)

    def local(src, dst, k):
        return pltpu.make_async_copy(src, dst, loc_sem.at[k])

    order = [lax.rem(g + r, GROUPS) for r in (0, 3, 1, 2)]
    cols = [pl.ds(pl.multiple_of(q * ROWS, 128), ROWS) for q in order]
    c_res = local(res_h.at[0], res_v, 0)
    c_sd = local(sdof_h.at[0, 0], sdof_v, 1)
    c_md = local(mdof_h.at[0, 0], mdof_v, 2)
    c_pair = local(pair_h.at[s, g], pair_s, 3)
    c_proj = [local(proj_h.at[0, 0, j], proj_v.at[j, pl.ds(0, FS)], 4 + j) for j in range(PAIRS)]
    c_z = local(zb_h.at[0, :, cols[0]], z_v, 8)
    c_ci = local(cinv_h, cinv_v, 9)
    c_y = [local(yb_h.at[0, :, cols[r]], y_v.at[r], 10 + r) for r in range(GROUPS)]
    c_n = [local(neu_h.at[0, :, cols[r]], neu_v.at[r], 14 + r) for r in range(GROUPS)]
    for c in [c_res, c_sd, c_md, c_pair] + c_proj + [c_z, c_ci] + c_y + c_n:
        c.start()

    idv_v[...] = jnp.full((8, 128), ids_s[0] * NC, jnp.int32)
    idin_v[0] = idv_v[...]
    c_res.wait()
    rbf_v[...] = res_v[...].astype(BF16)
    c_sd.wait()

    pl.semaphore_wait(barrier, SUBS - 1 + GROUPS - 1)

    def rcopy(src, dst, ss, rs, dev):
        return pltpu.make_async_remote_copy(
            src_ref=src, dst_ref=dst, send_sem=ss, recv_sem=rs, device_id=dev, device_id_type=MESH
        )

    sd = [
        rcopy(sdof_v, sdin_v.at[o], sd_send.at[o], sd_recv.at[o], sub_dev(-REACH[o]))
        for o in range(4)
    ]
    rs = [
        rcopy(rbf_v, rin_v.at[o], rs_send.at[o], rs_recv.at[o], sub_dev(-REACH[o]))
        for o in range(4)
    ]
    for o in range(4):
        sd[o].start()
    for o in (0, 3, 1, 2):
        rs[o].start()

    def idc(r):
        return rcopy(idv_v, idin_v.at[r], id_send.at[r], id_recv.at[r], sub_dev(r))

    def id_start(r, c):
        idc(r).start()
        return c

    lax.fori_loop(1, SUBS, id_start, 0)

    c_md.wait()
    for j in range(PAIRS):
        proj_v[j, pl.ds(FS, 16), :] = jnp.ones((16, FM), BF16)
    for j in range(PAIRS):
        c_proj[j].wait()

    def make_u(j, c):
        row = mdof_v[pl.ds(j, 1), :]
        for lo in range(0, ROWS, 256):
            w = min(256, ROWS - lo)
            at = lax.broadcasted_iota(jnp.int32, (w, FM), 0) + lo
            gt_v[pl.ds(0, w), :] = one_hot(at == row)
            u_v[j, :, pl.ds(lo, w)] = mm_nt(proj_v[j], gt_v[pl.ds(0, w), :]).astype(BF16)
        return c

    lax.fori_loop(0, PAIRS, make_u, 0)

    c_pair.wait()
    pos, face = [], []
    for j in range(PAIRS):
        e = lax.rem(pair_s[j, 0] - s + (2 + SUBS), SUBS)
        pos.append(e - lax.div(e, 3))
        face.append(pair_s[j, 1])

    for o in range(4):
        sd[o].wait_recv()
    for j in range(PAIRS):
        code = jnp.full((1, FS), pos[j] * 2 + face[j], jnp.int32)
        row = jnp.zeros((1, FS), jnp.int32)
        for k in range(8):
            row = row + jnp.where(code == k, sdin_v[k // 2, pl.ds(k % 2, 1), :], 0)
        for lo in range(0, ROWS, 128):
            at = lax.broadcasted_iota(jnp.int32, (128, FS), 0) + lo
            st_v[j, pl.ds(lo, 128), :] = one_hot(at == row)

    for o in range(4):
        rs[o].wait_recv()

    base_v[...] = res_v[...]
    for j in range(PAIRS):
        where_j = jnp.full((COLS, ROWS), pos[j], jnp.int32)
        near = rin_v[0] * one_hot(where_j == 0)
        for o in range(1, 4):
            near = near + rin_v[o] * one_hot(where_j == o)
        tr_v[...] = mm_nn(near, st_v[j]).astype(BF16)
        mask = u_v[j, pl.ds(FS, 16), :][0:1, :].astype(F32)
        mism = mm_nn(tr_v[...], u_v[j, pl.ds(0, FS), :]) - mask * res_v[...]
        base_v[...] += 0.5 * mism
        mm_v[...] = mism.astype(BF16)
        ret_v[...] = mm_nt(mm_v[...], u_v[j, pl.ds(0, FS), :]).astype(BF16)
        t_v[j] = mm_nt(ret_v[...], st_v[j])

    rp = [
        rcopy(reply_v.at[o], rpin_v.at[o], rp_send.at[o], rp_recv.at[o], sub_dev(REACH[o]))
        for o in range(4)
    ]
    for o in (0, 3, 1, 2):
        total = jnp.zeros((COLS, ROWS), F32)
        for j in range(PAIRS):
            here = jnp.full((COLS, ROWS), pos[j], jnp.int32) == o
            total = total + jnp.where(here, t_v[j], 0.0)
        reply_v[o] = total.astype(BF16)
        rp[o].start()

    def id_wait(r, c):
        idc(r).wait()
        return c

    lax.fori_loop(1, SUBS, id_wait, 0)
    gap = lax.broadcasted_iota(jnp.int32, (NC, CBLK * NC), 1) - lax.broadcasted_iota(
        jnp.int32, (NC, CBLK * NC), 0
    )

    def make_exp(r, c):
        exp_v[pl.ds(pl.multiple_of(r * NC, 16), NC), :] = one_hot(gap == idin_v[r][0:1, 0:1])
        return c

    lax.fori_loop(0, SUBS, make_exp, 0)
    c_ci.wait()
    my_id = jnp.full((NC, CBLK * NC), ids_s[0], jnp.int32)

    def add_rows(k, rows):
        return rows + jnp.where(my_id == k, cinv_v[pl.ds(pl.multiple_of(k * NC, 8), NC), :], 0.0)

    chi, clo = split(lax.fori_loop(0, CBLK, add_rows, jnp.zeros((NC, CBLK * NC), F32)))
    a_v[...] = mm_nt(jnp.concatenate([chi, clo], 0), exp_v[...]).astype(BF16)

    for r in range(GROUPS):
        c_y[r].wait()
        c_n[r].wait()
        yhi, ylo = split(y_v[r])
        t = mm_nt(jnp.concatenate([yhi, ylo], 0), neu_v[r])
        if r == 0:
            wacc_v[...] = t
        else:
            wacc_v[...] += t
    c_z.wait()
    whi, wlo = split(z_v[...] - wacc_v[0:NC, :] - wacc_v[NC:, :])
    wcat_v[0:NC, :] = whi
    wcat_v[NC : 2 * NC, :] = whi
    wcat_v[2 * NC :, :] = wlo

    for o in range(4):
        rp[o].wait_recv()
        base_v[...] -= 0.5 * rpin_v[o].astype(F32)
    rbf2, rlo2 = split(base_v[...])
    c_bal = local(base_v, bal_h.at[0], 18)
    c_bal.start()
    for o in range(4):
        rs[o].wait_send()
    rbf_v[...] = rbf2

    def half(ref, h):
        return ref.at[pl.ds(h * HALF, HALF)]

    def gcopy(src, slot, h, k, step):
        return rcopy(half(src, h), half(gath_v.at[slot], h), g_send.at[k], g_recv.at[k], grp_dev(step))

    up0 = gcopy(rbf_v, 0, 0, 0, 1)
    dn1 = gcopy(rbf_v, 1, 1, 1, 3)
    up1 = gcopy(rbf_v, 0, 1, 2, 1)
    dn0 = gcopy(rbf_v, 1, 0, 3, 3)
    fup = gcopy(gath_v.at[0], 2, 0, 4, 1)
    fdn = gcopy(gath_v.at[1], 2, 1, 5, 3)
    up0.start()
    dn1.start()
    up1.start()
    dn0.start()

    zhi, zlo = split(z_v[...])
    p2 = mm_nt(jnp.concatenate([zhi, zlo], 0), rbf2)
    part_v[0] = (p2[:NC] + p2[NC:] + mm_nt(zhi, rlo2)).astype(BF16)

    def ptc(r):
        return rcopy(part_v.at[0], part_v.at[r], pt_send.at[r], pt_recv.at[r], sub_dev(r))

    def pt_start(r, c):
        ptc(r).start()
        return c

    lax.fori_loop(1, SUBS, pt_start, 0)
    acc_v[...] = mm_nt(rbf_v[...], neu_v[0])

    up0.wait_recv()
    fup.start()
    dn1.wait_recv()
    fdn.start()

    def pt_wait(r, c):
        ptc(r).wait()
        return c

    lax.fori_loop(1, SUBS, pt_wait, 0)
    parts = part_v[...].reshape(SUBS * NC, COLS)
    m2 = mm_nn(a_v[...], parts)
    m_v[0] = m2[:NC] + m2[NC:]

    mc = [rcopy(m_v.at[0], m_v.at[r], m_send.at[r], m_recv.at[r], grp_dev(r)) for r in range(1, 4)]
    for c in mc:
        c.start()

    up1.wait_recv()
    acc_v[...] += mm_nt(gath_v[0], neu_v[1])
    dn0.wait_recv()
    acc_v[...] += mm_nt(gath_v[1], neu_v[2])
    for c in mc:
        c.wait()
    mhi, mlo = split((m_v[0] + m_v[1] + m_v[2] + m_v[3]).T)
    mcat = jnp.concatenate([mhi, mlo, mhi], 1)
    acc_v[...] += mm_nn(mcat, wcat_v[...])
    fup.wait_recv()
    fdn.wait_recv()
    acc_v[...] += mm_nt(gath_v[2], neu_v[3])
    c_cor = local(acc_v, cor_h.at[0], 19)
    c_cor.start()
    for c in sd + rp + [up0, dn1, up1, dn0, fup, fdn]:
        c.wait_send()
    c_bal.wait()
    c_cor.wait()


def local_part(
    residual, neumann, projection, pair_list, slave_dofs, master_dofs, zbasis, ybasis, coarse_inverse, coarse_ids
):
    any_spec = pl.BlockSpec(memory_space=pl.ANY)
    smem_spec = pl.BlockSpec(memory_space=pltpu.SMEM)
    dma = pltpu.SemaphoreType.DMA
    vm = pltpu.VMEM
    region = jax.ShapeDtypeStruct((1, COLS, ROWS), F32)
    scratch = [
        pltpu.SMEM((PAIRS, 2), jnp.int32),
        vm((COLS, ROWS), F32),
        vm((COLS, ROWS), BF16),
        vm((4, COLS, ROWS), BF16),
        vm((2, FS), jnp.int32),
        vm((4, 2, FS), jnp.int32),
        vm((PAIRS, FM), jnp.int32),
        vm((PAIRS, EXT, FM), BF16),
        vm((PAIRS, EXT, ROWS), BF16),
        vm((PAIRS, ROWS, FS), BF16),
        vm((256, FM), BF16),
        vm((GROUPS, ROWS, ROWS), BF16),
        vm((NC, ROWS), F32),
        vm((GROUPS, NC, ROWS), F32),
        vm((CBLK * NC, CBLK * NC), F32),
        vm((8, 128), jnp.int32),
        vm((SUBS, 8, 128), jnp.int32),
        vm((SUBS * NC, CBLK * NC), BF16),
        vm((2 * NC, SUBS * NC), BF16),
        vm((SUBS, NC, COLS), BF16),
        vm((GROUPS, NC, COLS), F32),
        vm((3 * NC, ROWS), BF16),
        vm((2 * NC, ROWS), F32),
        vm((COLS, ROWS), F32),
        vm((COLS, FS), BF16),
        vm((COLS, ROWS), BF16),
        vm((COLS, FS), BF16),
        vm((PAIRS, COLS, ROWS), F32),
        vm((4, COLS, ROWS), BF16),
        vm((4, COLS, ROWS), BF16),
        vm((3, COLS, ROWS), BF16),
        vm((COLS, ROWS), F32),
        dma((20,)),
        dma((4,)), dma((4,)), dma((4,)), dma((4,)), dma((4,)), dma((4,)),
        dma((SUBS,)), dma((SUBS,)), dma((SUBS,)), dma((SUBS,)),
        dma((6,)), dma((6,)), dma((4,)), dma((4,)),
    ]
    return pl.pallas_call(
        kernel,
        out_shape=(region, region),
        in_specs=[any_spec, smem_spec] + [any_spec] * 8,
        out_specs=(any_spec, any_spec),
        scratch_shapes=scratch,
        compiler_params=pltpu.CompilerParams(
            collective_id=0, has_side_effects=True, vmem_limit_bytes=60 * 1024 * 1024
        ),
    )(
        pair_list, coarse_ids, residual, neumann, projection, slave_dofs, master_dofs, zbasis, ybasis, coarse_inverse
    )


def solution(mesh):
    placed = (
        P("sub", None, "grp"),
        P("sub", "grp", None),
        P("sub", "grp", None, None, None),
        P(),
        P("sub", "grp", None, None),
        P("sub", "grp", None, None),
        P("sub", None, None),
        P("sub", None, None),
        P(),
        P("sub"),
    )
    return jax.shard_map(
        local_part,
        mesh=mesh,
        in_specs=placed,
        out_specs=(P("sub", None, "grp"), P("sub", None, "grp")),
        check_vma=False,
    )
```

```python
import jax
import jax.numpy as jnp
from jax import lax
from jax.experimental import pallas as pl
from jax.experimental.pallas import tpu as pltpu
from jax.sharding import PartitionSpec as P

FS = 768
FM = 1024
NC = 48
COLS = 128
PAIRS = 4
ROWS = 1152
SUBS = 32
GROUPS = 4
CBLK = 16
REACH = (-2, -1, 1, 2)
HALF = COLS // 2
CHUNKS = 3
CW = ROWS // CHUNKS
ROW = 8
PLANES = SUBS // ROW
CHIPS = SUBS // 2
F32 = jnp.float32
BF16 = jnp.bfloat16
I32 = jnp.int32
MESH = pl.DeviceIdType.MESH


def mm_nn(a, b):
    return lax.dot_general(a, b, (((1,), (0,)), ((), ())), preferred_element_type=F32)


def mm_nt(a, b):
    return lax.dot_general(a, b, (((1,), (1,)), ((), ())), preferred_element_type=F32)


def split(x):
    hi = x.astype(BF16)
    return hi, (x - hi.astype(F32)).astype(BF16)


def one_hot(cond):
    return jnp.where(cond, 1.0, 0.0).astype(BF16)


def kernel(
    pair_h, ids_s, res_h, neu_h, proj_h, sdof_h, mdof_h, zb_h, yb_h, cinv_h,
    bal_h, cor_h,
    pair_v, res_v, rbf_v, lhs_v, rin_v, sdof_v, sdin_v, mdof_v, proj_v, gt_v, rg_v, zg_v, st_v,
    zsf_v, zsin_v, neu_v, z_v, y_v, cinv_v, idrow_v, idcol_v, ecol_v, erow_v, t1_v, a_v,
    c_v, cin_v, col_v, pxo_v, pxi_v, m_v, wcat_v, wacc_v, w32_v, w16_v, v32_v, v16_v,
    base_v, part_v, tr_v, mm_v, ret_v, t_v, ab32_v, ab_v, cd_v, sw_v, sum_v, rpin_v, bal_v, gath_v, acc_v,
    loc_sem, sd_send, sd_recv, zs_send, zs_recv, c_send, c_recv, p1_send, p1_recv, fw_send, fw_recv,
    sw_send, sw_recv, cd_send, cd_recv, ab_send, ab_recv,
    ix_send, ix_recv, iz_send, iz_recv, px_send, px_recv, pz_send, pz_recv,
    g_send, g_recv, m_send, m_recv,
):
    s = lax.axis_index("sub")
    g = lax.axis_index("grp")
    core = lax.rem(s, 2)
    chip = lax.div(s, 2)
    row = lax.rem(s, ROW)

    def sub_dev(step):
        return (lax.rem(s + step + SUBS, SUBS), g)

    def chip_dev(step, c):
        return (lax.rem(chip + step + CHIPS, CHIPS) * 2 + c, g)

    def row_dev(r):
        return (s - row + lax.rem(row + r, ROW), g)

    def grp_dev(step):
        return (s, lax.rem(g + step, GROUPS))

    mate = (s + 1 - 2 * core, g)

    barrier = pltpu.get_barrier_semaphore()
    greeted = [sub_dev(k) for k in REACH] + [row_dev(r) for r in range(1, ROW)]
    greeted += [sub_dev(ROW * k) for k in range(1, PLANES)] + [grp_dev(k) for k in range(1, GROUPS)]
    for dev in greeted:
        pl.semaphore_signal(barrier, inc=1, device_id=dev, device_id_type=MESH)

    def local(src, dst, k):
        return pltpu.make_async_copy(src, dst, loc_sem.at[k])

    order = [lax.rem(g + r, GROUPS) for r in (0, 3, 1, 2)]
    cols = [pl.ds(pl.multiple_of(q * ROWS, 128), ROWS) for q in order]
    c_res = local(res_h.at[0], res_v, 0)
    c_sd = local(sdof_h.at[0, 0], sdof_v, 1)
    c_md = local(mdof_h.at[0, 0], mdof_v, 2)
    c_pair = local(pair_h.at[g], pair_v, 3)
    c_proj = [local(proj_h.at[0, 0, j], proj_v.at[j], 4 + j) for j in range(PAIRS)]
    c_z = local(zb_h.at[0, :, cols[0]], z_v, 8)
    c_ci = local(cinv_h, cinv_v, 9)
    c_y = [local(yb_h.at[0, :, cols[r]], y_v.at[r], 10 + r) for r in range(GROUPS)]
    c_n = [local(neu_h.at[0, :, cols[r]], neu_v.at[r], 14 + r) for r in range(GROUPS)]
    for c in [c_res, c_sd, c_md, c_pair, c_z] + c_proj + [c_ci] + c_y + c_n:
        c.start()

    idrow_v[0] = jnp.full((8, 128), ids_s[0] * NC, I32)
    idcol_v[0] = idrow_v[0]
    c_res.wait()
    rbf_v[...] = res_v[...].astype(BF16)
    c_sd.wait()

    pl.semaphore_wait(barrier, len(greeted))

    def rcopy(src, dst, ss, rs, dev):
        return pltpu.make_async_remote_copy(
            src_ref=src, dst_ref=dst, send_sem=ss, recv_sem=rs, device_id=dev, device_id_type=MESH
        )

    def half(ref, h):
        return ref.at[pl.ds(pl.multiple_of(h * HALF, HALF), HALF)]

    sd = [
        rcopy(sdof_v, sdin_v.at[o], sd_send.at[o], sd_recv.at[o], sub_dev(-REACH[o]))
        for o in range(4)
    ]
    shared_step = 2 * core - 1
    p1 = [
        rcopy(half(rbf_v, h), half(rin_v.at[1 - core], h), p1_send.at[h], p1_recv.at[1 - core],
              chip_dev(shared_step, h))
        for h in range(2)
    ]
    p1.append(rcopy(rbf_v, rin_v.at[2], p1_send.at[2], p1_recv.at[2], chip_dev(-shared_step, core)))
    p1.append(rcopy(rbf_v, rin_v.at[3], p1_send.at[3], p1_recv.at[3], mate))
    for c in sd + p1:
        c.start()

    ix = [rcopy(idrow_v.at[0], idrow_v.at[r], ix_send.at[r], ix_recv.at[r], row_dev(r)) for r in range(1, ROW)]
    iz = [
        rcopy(idcol_v.at[0], idcol_v.at[k], iz_send.at[k], iz_recv.at[k], sub_dev(ROW * k))
        for k in range(1, PLANES)
    ]
    for c in ix + iz:
        c.start()

    c_z.wait()
    zhi, zlo = split(z_v[...])
    lhs_v[0:COLS, :] = rbf_v[...]
    lhs_v[COLS : 2 * COLS, :] = (res_v[...] - rbf_v[...].astype(F32)).astype(BF16)
    lhs_v[2 * COLS : 2 * COLS + NC, :] = zhi
    lhs_v[2 * COLS + NC :, :] = zlo
    at_face = lax.broadcasted_iota(I32, (ROWS, FS), 0)
    for f in range(2):
        st_v[f] = one_hot(at_face == sdof_v[pl.ds(f, 1), :])
        zsf_v[f] = mm_nn(lhs_v[2 * COLS : 2 * COLS + NC, :], st_v[f]).astype(BF16)
    zs = [
        rcopy(zsf_v, zsin_v.at[o], zs_send.at[o], zs_recv.at[o], sub_dev(-REACH[o])) for o in range(4)
    ]
    for c in zs:
        c.start()

    c_pair.wait()
    lane = lax.broadcasted_iota(I32, (1, SUBS), 1)

    def entry(j, k):
        line = pair_v[j, pl.ds(k, 1), :].astype(F32)
        return jnp.sum(jnp.where(lane == s, line, 0.0), axis=1, keepdims=True).astype(I32)

    near = [(entry(j, 0) - s + (SUBS + 2)) & (SUBS - 1) for j in range(PAIRS)]
    face = [entry(j, 1) for j in range(PAIRS)]
    slot_e = [1 - core, 4 - core, 4 * core, 3 - 2 * core]
    for j in range(PAIRS):
        here = jnp.broadcast_to(near[j], (16, 128))
        side = jnp.broadcast_to(face[j], (16, 128))
        for q in range(4):
            hot = jnp.where(here == slot_e[q], 1.0, 0.0)
            w32_v[j, q] = hot[0:8]
            w16_v[j, q] = hot.astype(BF16)
            hot = jnp.where(here == REACH[q] + 2, 1.0, 0.0)
            v32_v[j, q] = hot[0:8]
            for k in range(2):
                v16_v[j, q, k] = jnp.where(side == k, hot, 0.0).astype(BF16)

    c_md.wait()

    def make_g(j, c):
        line = mdof_v[pl.ds(j, 1), :]
        gt_v[j] = one_hot(lax.broadcasted_iota(I32, (ROWS, FM), 0) == line)
        for lo in range(0, FM, 256):
            w = pl.ds(lo, 256)
            got = mm_nn(lhs_v[...], gt_v[j, :, w])
            rg_v[j, :, w] = got[0:COLS] + got[COLS : 2 * COLS]
            zg_v[j, :, w] = got[2 * COLS :].astype(BF16)
        return c

    lax.fori_loop(0, PAIRS, make_g, 0)
    res_part = mm_nt(lhs_v[2 * COLS :, :], rbf_v[...])
    part_v[...] = res_part[:NC] + res_part[NC:] + mm_nt(
        lhs_v[2 * COLS : 2 * COLS + NC, :], lhs_v[COLS : 2 * COLS, :]
    )

    for c in sd:
        c.wait_recv()
    for j in range(PAIRS):
        code = jnp.broadcast_to(near[j] * 2 + face[j], (1, FS))
        line = jnp.zeros((1, FS), I32)
        for o in range(4):
            for k in range(2):
                line = line + jnp.where(code == (REACH[o] + 2) * 2 + k, sdin_v[o, pl.ds(k, 1), :], 0)
        st_v[j] = one_hot(at_face == line)

    for c in ix + iz:
        c.wait()
    gap = lax.broadcasted_iota(I32, (NC, CBLK * NC), 1) - lax.broadcasted_iota(I32, (NC, CBLK * NC), 0)
    for k in range(PLANES):
        ecol_v[k * NC : (k + 1) * NC, :] = one_hot(gap == idcol_v[k][0:1, 0:1])
    for r in range(ROW):
        erow_v[r * NC : (r + 1) * NC, :] = one_hot(gap == idrow_v[(ROW - r) % ROW][0:1, 0:1])
    c_ci.wait()
    chi, clo = split(cinv_v[...])
    t1_v[0] = mm_nt(chi, ecol_v[...]).astype(BF16)
    t1_v[1] = mm_nt(clo, ecol_v[...]).astype(BF16)
    for k in range(2):
        a_v[k] = mm_nn(erow_v[...], t1_v[k]).astype(BF16)

    fw = [
        rcopy(half(rin_v.at[q], core), half(rin_v.at[q], core), fw_send.at[q], fw_recv.at[q], mate)
        for q in range(2)
    ]
    got = [
        rcopy(half(rbf_v, 0), half(rin_v.at[q], core), p1_send.at[0], p1_recv.at[q], mate) for q in range(2)
    ]
    for q in range(2):
        got[q].wait_recv()
        fw[q].start()
    for c in c_proj:
        c.wait()
    p1[2].wait_recv()
    p1[3].wait_recv()
    for q in range(2):
        fw[q].wait_recv()

    for j in range(PAIRS):
        there = rin_v[0] * jnp.tile(w16_v[j, 0], (8, 9))
        for q in range(1, 4):
            there = there + rin_v[q] * jnp.tile(w16_v[j, q], (8, 9))
        tr_v[j] = mm_nn(there, st_v[j]).astype(BF16)
    for j in range(PAIRS):
        mhi, mlo = split(mm_nn(tr_v[j], proj_v[j]) - rg_v[j])
        mm_v[j, 0:COLS, :] = mhi
        mm_v[j, COLS:, :] = mlo
        ret_v[j] = mm_nt(mhi, proj_v[j]).astype(BF16)

    for c in zs:
        c.wait_recv()
    cc = [rcopy(c_v.at[o], cin_v.at[o], c_send.at[o], c_recv.at[o], sub_dev(REACH[o])) for o in range(4)]
    shares = []
    for j in range(PAIRS):
        zsel = jnp.zeros((NC, FS), BF16)
        for o in range(4):
            for k in range(2):
                zsel = zsel + zsin_v[o, k] * jnp.tile(v16_v[j, o, k], (3, 6))
        shares.append(mm_nt(zsel, ret_v[j]))
    for o in range(4):
        total = shares[0] * jnp.tile(v32_v[0, o], (6, 1))
        for j in range(1, PAIRS):
            total = total + shares[j] * jnp.tile(v32_v[j, o], (6, 1))
        c_v[o] = (-0.5 * total).astype(BF16)
        cc[o].start()

    swc, cdc, abc = [], [], []
    for ch in range(CHUNKS):
        swc.append(rcopy(ab_v.at[ch, 1 - core], sw_v.at[ch], sw_send.at[ch], sw_recv.at[ch], mate))
        cdc.append([
            rcopy(cd_v.at[ch, 0], rpin_v.at[1, ch], cd_send.at[ch, 0], cd_recv.at[ch, 0],
                  chip_dev(shared_step, core)),
            rcopy(cd_v.at[ch, 1], rpin_v.at[2, ch], cd_send.at[ch, 1], cd_recv.at[ch, 1], mate),
        ])
        abc.append([
            rcopy(sum_v.at[ch, q], half(rpin_v.at[0, ch], core), ab_send.at[ch, q], ab_recv.at[ch, core],
                  chip_dev(2 * q - 1, 1 - q))
            for q in range(2)
        ])

    def add_swapped(ch):
        swc[ch].wait_recv()
        for q in range(2):
            mine = ab32_v[ch, q, pl.ds(pl.multiple_of(core * HALF, HALF), HALF), :]
            sum_v[ch, q] = (mine + sw_v[ch, q].astype(F32)).astype(BF16)
            abc[ch][q].start()

    for ch in range(CHUNKS):
        for j in range(PAIRS):
            t_v[j] = mm_nt(ret_v[j], st_v[j, pl.ds(ch * CW, CW), :])
        for q in range(4):
            total = t_v[0] * jnp.tile(w32_v[0, q], (16, 3))
            for j in range(1, PAIRS):
                total = total + t_v[j] * jnp.tile(w32_v[j, q], (16, 3))
            if q < 2:
                ab32_v[ch, q] = total
                for h in range(2):
                    ab_v[ch, h, q] = total[h * HALF : (h + 1) * HALF].astype(BF16)
            else:
                cd_v[ch, q - 2] = total.astype(BF16)
            if q == 1:
                swc[ch].start()
        cdc[ch][0].start()
        cdc[ch][1].start()
        if ch > 0:
            add_swapped(ch - 1)
    add_swapped(CHUNKS - 1)

    def scatter(ch):
        at = pl.ds(ch * CW, CW)
        moved = mm_nt(mm_v[0], gt_v[0, at, :])
        for j in range(1, PAIRS):
            moved = moved + mm_nt(mm_v[j], gt_v[j, at, :])
        base_v[:, at] = res_v[:, at] + 0.5 * (moved[:COLS] + moved[COLS:])

    scatter(0)

    part = jnp.zeros((2 * NC, 2 * COLS), F32)
    for j in range(PAIRS):
        part = part + mm_nt(zg_v[j], mm_v[j])
    part = part_v[...] + 0.5 * (part[:NC, :COLS] + part[NC:, :COLS] + part[:NC, COLS:])
    for o in range(4):
        cc[o].wait_recv()
        part = part + cin_v[o].astype(F32)
    col_v[0] = part.astype(BF16)
    pz = [
        rcopy(col_v.at[0], col_v.at[k], pz_send.at[k], pz_recv.at[k], sub_dev(ROW * k))
        for k in range(1, PLANES)
    ]
    for c in pz:
        c.start()

    def gcopy(src, ch, slot, h, k, step):
        return rcopy(half(src, h), half(gath_v.at[slot, ch], h), g_send.at[ch, k], g_recv.at[ch, k], grp_dev(step))

    gat = []
    for ch in range(CHUNKS):
        gat.append([
            gcopy(bal_v.at[ch], ch, 0, 0, 0, 1),
            gcopy(bal_v.at[ch], ch, 1, 1, 1, 3),
            gcopy(bal_v.at[ch], ch, 0, 1, 2, 1),
            gcopy(bal_v.at[ch], ch, 1, 0, 3, 3),
            gcopy(gath_v.at[0, ch], ch, 2, 0, 4, 1),
            gcopy(gath_v.at[1, ch], ch, 2, 1, 5, 3),
        ])

    def balance(ch):
        at = pl.ds(ch * CW, CW)
        cdc[ch][0].wait_recv()
        cdc[ch][1].wait_recv()
        for h in range(2):
            rcopy(sum_v.at[ch, 0], half(rpin_v.at[0, ch], h), ab_send.at[ch, 0], ab_recv.at[ch, h], mate).wait_recv()
        back = rpin_v[0, ch].astype(F32) + rpin_v[1, ch].astype(F32) + rpin_v[2, ch].astype(F32)
        new = base_v[:, at] - 0.5 * back
        base_v[:, at] = new
        bal_v[ch] = new.astype(BF16)
        for k in range(4):
            gat[ch][k].start()

    def forward(ch):
        gat[ch][0].wait_recv()
        gat[ch][4].start()
        gat[ch][1].wait_recv()
        gat[ch][5].start()

    def solve(block, ch, x):
        return mm_nt(x, neu_v[block, :, pl.ds(ch * CW, CW)])

    balance(0)
    scatter(1)
    balance(1)
    scatter(2)

    for c in pz:
        c.wait()
    column = col_v[...].reshape(PLANES * NC, COLS)
    made = (mm_nn(a_v[0], column) + mm_nn(a_v[1], column)).astype(BF16)
    for r in range(ROW):
        pxo_v[r] = made[r * NC : (r + 1) * NC]
    px = [rcopy(pxo_v.at[r], pxi_v.at[r], px_send.at[r], px_recv.at[r], row_dev(r)) for r in range(1, ROW)]
    for c in px:
        c.start()
    balance(2)
    c_bal = local(base_v, bal_h.at[0], 18)
    c_bal.start()

    for r in range(GROUPS):
        c_y[r].wait()
        c_n[r].wait()
        yhi, ylo = split(y_v[r])
        t = mm_nt(jnp.concatenate([yhi, ylo], 0), neu_v[r])
        if r == 0:
            wacc_v[...] = t
        else:
            wacc_v[...] += t
    whi, wlo = split(z_v[...] - wacc_v[0:NC, :] - wacc_v[NC:, :])
    wcat_v[0:NC, :] = whi
    wcat_v[NC : 2 * NC, :] = whi
    wcat_v[2 * NC :, :] = wlo

    forward(0)
    forward(1)
    mine = pxo_v[0].astype(F32)
    for r in range(1, ROW):
        px[r - 1].wait()
        mine = mine + pxi_v[r].astype(F32)
    m_v[0] = mine
    mc = [rcopy(m_v.at[0], m_v.at[r], m_send.at[r], m_recv.at[r], grp_dev(r)) for r in range(1, 4)]
    for c in mc:
        c.start()
    acc_v[...] = solve(0, 0, bal_v[0])
    acc_v[...] += solve(0, 1, bal_v[1])
    forward(2)
    acc_v[...] += solve(0, 2, bal_v[2])
    for ch in range(CHUNKS):
        for q in range(2):
            gat[ch][2 + q].wait_recv()
            acc_v[...] += solve(1 + q, ch, gath_v[q, ch])
    for c in mc:
        c.wait()
    mhi, mlo = split((m_v[0] + m_v[1] + m_v[2] + m_v[3]).T)
    acc_v[...] += mm_nn(jnp.concatenate([mhi, mlo, mhi], 1), wcat_v[...])
    for ch in range(CHUNKS):
        gat[ch][4].wait_recv()
        gat[ch][5].wait_recv()
        acc_v[...] += solve(3, ch, gath_v[2, ch])
    c_cor = local(acc_v, cor_h.at[0], 19)
    c_cor.start()
    for c in sd + zs + cc + p1 + fw + swc:
        c.wait_send()
    for ch in range(CHUNKS):
        for c in cdc[ch] + abc[ch] + gat[ch]:
            c.wait_send()
    c_bal.wait()
    c_cor.wait()


def hand_over(a_ref, b_ref, x_ref, y_ref):
    x_ref[...] = a_ref[...]
    y_ref[...] = b_ref[...]


def local_part(
    residual, neumann, projection, pair_list, slave_dofs, master_dofs, zbasis, ybasis, coarse_inverse, coarse_ids
):
    any_spec = pl.BlockSpec(memory_space=pl.ANY)
    smem_spec = pl.BlockSpec(memory_space=pltpu.SMEM)
    dma = pltpu.SemaphoreType.DMA
    vm = pltpu.VMEM
    region = jax.ShapeDtypeStruct((1, COLS, ROWS), F32)
    scratch = [
        vm((PAIRS, 2, SUBS), I32),
        vm((COLS, ROWS), F32),
        vm((COLS, ROWS), BF16),
        vm((2 * COLS + 2 * NC, ROWS), BF16),
        vm((4, COLS, ROWS), BF16),
        vm((2, FS), I32),
        vm((4, 2, FS), I32),
        vm((PAIRS, FM), I32),
        vm((PAIRS, FS, FM), BF16),
        vm((PAIRS, ROWS, FM), BF16),
        vm((PAIRS, COLS, FM), F32),
        vm((PAIRS, 2 * NC, FM), BF16),
        vm((PAIRS, ROWS, FS), BF16),
        vm((2, NC, FS), BF16),
        vm((4, 2, NC, FS), BF16),
        vm((GROUPS, ROWS, ROWS), BF16),
        vm((NC, ROWS), F32),
        vm((GROUPS, NC, ROWS), F32),
        vm((CBLK * NC, CBLK * NC), F32),
        vm((ROW, 8, 128), I32),
        vm((PLANES, 8, 128), I32),
        vm((PLANES * NC, CBLK * NC), BF16),
        vm((ROW * NC, CBLK * NC), BF16),
        vm((2, CBLK * NC, PLANES * NC), BF16),
        vm((2, ROW * NC, PLANES * NC), BF16),
        vm((4, NC, COLS), BF16),
        vm((4, NC, COLS), BF16),
        vm((PLANES, NC, COLS), BF16),
        vm((ROW, NC, COLS), BF16),
        vm((ROW, NC, COLS), BF16),
        vm((GROUPS, NC, COLS), F32),
        vm((3 * NC, ROWS), BF16),
        vm((2 * NC, ROWS), F32),
        vm((PAIRS, 4, 8, 128), F32),
        vm((PAIRS, 4, 16, 128), BF16),
        vm((PAIRS, 4, 8, 128), F32),
        vm((PAIRS, 4, 2, 16, 128), BF16),
        vm((COLS, ROWS), F32),
        vm((NC, COLS), F32),
        vm((PAIRS, COLS, FS), BF16),
        vm((PAIRS, 2 * COLS, FM), BF16),
        vm((PAIRS, COLS, FS), BF16),
        vm((PAIRS, COLS, CW), F32),
        vm((CHUNKS, 2, COLS, CW), F32),
        vm((CHUNKS, 2, 2, HALF, CW), BF16),
        vm((CHUNKS, 2, COLS, CW), BF16),
        vm((CHUNKS, 2, HALF, CW), BF16),
        vm((CHUNKS, 2, HALF, CW), BF16),
        vm((3, CHUNKS, COLS, CW), BF16),
        vm((CHUNKS, COLS, CW), BF16),
        vm((3, CHUNKS, COLS, CW), BF16),
        vm((COLS, ROWS), F32),
        dma((20,)),
        dma((4,)), dma((4,)), dma((4,)), dma((4,)), dma((4,)), dma((4,)),
        dma((4,)), dma((4,)), dma((2,)), dma((2,)),
        dma((CHUNKS,)), dma((CHUNKS,)), dma((CHUNKS, 2)), dma((CHUNKS, 2)), dma((CHUNKS, 2)), dma((CHUNKS, 2)),
        dma((ROW,)), dma((ROW,)), dma((PLANES,)), dma((PLANES,)),
        dma((ROW,)), dma((ROW,)), dma((PLANES,)), dma((PLANES,)),
        dma((CHUNKS, 6)), dma((CHUNKS, 6)), dma((4,)), dma((4,)),
    ]
    outs = pl.pallas_call(
        kernel,
        out_shape=(region, region),
        in_specs=[any_spec, smem_spec] + [any_spec] * 8,
        out_specs=(any_spec, any_spec),
        scratch_shapes=scratch,
        compiler_params=pltpu.CompilerParams(
            collective_id=0, has_side_effects=True, vmem_limit_bytes=60 * 1024 * 1024
        ),
    )(
        jnp.transpose(pair_list, (1, 2, 3, 0)), coarse_ids, residual, neumann, projection,
        slave_dofs, master_dofs, zbasis, ybasis, coarse_inverse,
    )
    whole = pl.BlockSpec(memory_space=pltpu.VMEM)
    return pl.pallas_call(
        hand_over,
        out_shape=(region, region),
        in_specs=[whole, whole],
        out_specs=(whole, whole),
    )(*outs)


def solution(mesh):
    placed = (
        P("sub", None, "grp"),
        P("sub", "grp", None),
        P("sub", "grp", None, None, None),
        P(),
        P("sub", "grp", None, None),
        P("sub", "grp", None, None),
        P("sub", None, None),
        P("sub", None, None),
        P(),
        P("sub"),
    )
    return jax.shard_map(
        local_part,
        mesh=mesh,
        in_specs=placed,
        out_specs=(P("sub", None, "grp"), P("sub", None, "grp")),
        check_vma=False,
    )
```

```python
import jax
import jax.numpy as jnp
from jax import lax
from jax.experimental import pallas as pl
from jax.experimental.pallas import tpu as pltpu
from jax.sharding import PartitionSpec as P

FS = 768
FM = 1024
NC = 48
COLS = 128
PAIRS = 4
ROWS = 1152
SUBS = 32
GROUPS = 4
CBLK = 16
REACH = (-2, -1, 1, 2)
HALF = COLS // 2
CHUNKS = 3
CW = ROWS // CHUNKS
ROW = 8
PLANES = SUBS // ROW
CHIPS = SUBS // 2
F32 = jnp.float32
BF16 = jnp.bfloat16
I32 = jnp.int32
MESH = pl.DeviceIdType.MESH


def mm_nn(a, b):
    return lax.dot_general(a, b, (((1,), (0,)), ((), ())), preferred_element_type=F32)


def mm_nt(a, b):
    return lax.dot_general(a, b, (((1,), (1,)), ((), ())), preferred_element_type=F32)


def split(x):
    hi = x.astype(BF16)
    return hi, (x - hi.astype(F32)).astype(BF16)


def one_hot(cond):
    return jnp.where(cond, 1.0, 0.0).astype(BF16)


def kernel(
    pair_h, ids_s, res_h, neu_h, proj_h, sdof_h, mdof_h, zb_h, yb_h, cinv_h,
    bal_h, cor_h,
    pair_v, res_v, rbf_v, lhs_v, rin_v, sdof_v, sdin_v, mdof_v, proj_v, gt_v, rg_v, zg_v, st_v,
    zsf_v, zsin_v, neu_v, z_v, y_v, cinv_v, idrow_v, idcol_v, ecol_v, erow_v, t1_v, a_v,
    c_v, cin_v, col_v, pxo_v, pxi_v, m_v, w_v, zt_v, accy_v, w32_v, w16_v, v32_v, v16_v,
    base_v, part_v, tr_v, mm_v, ret_v, t_v, ab32_v, ab_v, cd_v, sw_v, sum_v, rpin_v, x_v, acc_v, cor_v,
    loc_sem, sd_send, sd_recv, zs_send, zs_recv, c_send, c_recv, p1_send, p1_recv, fw_send, fw_recv,
    sw_send, sw_recv, cd_send, cd_recv, ab_send, ab_recv,
    ix_send, ix_recv, iz_send, iz_recv, px_send, px_recv, pz_send, pz_recv,
    g_send, g_recv, m_send, m_recv,
):
    s = lax.axis_index("sub")
    g = lax.axis_index("grp")
    core = lax.rem(s, 2)
    chip = lax.div(s, 2)
    row = lax.rem(s, ROW)

    def sub_dev(step):
        return (lax.rem(s + step + SUBS, SUBS), g)

    def chip_dev(step, c):
        return (lax.rem(chip + step + CHIPS, CHIPS) * 2 + c, g)

    def row_dev(r):
        return (s - row + lax.rem(row + r, ROW), g)

    def grp_dev(step):
        return (s, lax.rem(g + step, GROUPS))

    mate = (s + 1 - 2 * core, g)

    def local(src, dst, k):
        return pltpu.make_async_copy(src, dst, loc_sem.at[k])

    c_res = local(res_h.at[0], res_v, 0)
    c_sd = local(sdof_h.at[0, 0], sdof_v, 1)
    c_res.start()
    c_sd.start()

    barrier = pltpu.get_barrier_semaphore()
    greeted = [row_dev(r) for r in range(1, ROW)]
    greeted += [sub_dev(ROW * k) for k in range(1, PLANES)] + [grp_dev(k) for k in range(1, GROUPS)]
    expected = len(greeted)
    for k in REACH:
        outside = (row + k < 0) if k < 0 else (row + k >= ROW)
        expected = expected + jnp.where(outside, 1, 0)

        @pl.when(outside)
        def _():
            pl.semaphore_signal(barrier, inc=1, device_id=sub_dev(k), device_id_type=MESH)

    for dev in greeted:
        pl.semaphore_signal(barrier, inc=1, device_id=dev, device_id_type=MESH)

    order = [lax.rem(g + r, GROUPS) for r in (0, 3, 1, 2)]
    cols = [pl.ds(pl.multiple_of(q * ROWS, 128), ROWS) for q in order]
    c_md = local(mdof_h.at[0, 0], mdof_v, 2)
    c_pair = local(pair_h.at[g], pair_v, 3)
    c_proj = [local(proj_h.at[0, 0, j], proj_v.at[j], 4 + j) for j in range(PAIRS)]
    c_z = local(zb_h.at[0, :, cols[0]], z_v, 8)
    c_ci = local(cinv_h, cinv_v, 9)
    c_y = [local(yb_h.at[0, :, cols[r]], y_v.at[r], 10 + r) for r in range(GROUPS)]
    c_n = [local(neu_h.at[0, :, cols[r]], neu_v.at[r], 14 + r) for r in range(GROUPS)]
    c_res.wait()
    rbf_v[...] = res_v[...].astype(BF16)
    c_sd.wait()

    pl.semaphore_wait(barrier, expected)

    def rcopy(src, dst, ss, rs, dev):
        return pltpu.make_async_remote_copy(
            src_ref=src, dst_ref=dst, send_sem=ss, recv_sem=rs, device_id=dev, device_id_type=MESH
        )

    def half(ref, h):
        return ref.at[pl.ds(pl.multiple_of(h * HALF, HALF), HALF)]

    sd = [
        rcopy(sdof_v, sdin_v.at[o], sd_send.at[o], sd_recv.at[o], sub_dev(-REACH[o]))
        for o in range(4)
    ]
    shared_step = 2 * core - 1
    p1 = [
        rcopy(half(rbf_v, h), half(rin_v.at[1 - core], h), p1_send.at[h], p1_recv.at[1 - core],
              chip_dev(shared_step, h))
        for h in range(2)
    ]
    p1.append(rcopy(rbf_v, rin_v.at[2], p1_send.at[2], p1_recv.at[2], chip_dev(-shared_step, core)))
    p1.append(rcopy(rbf_v, rin_v.at[3], p1_send.at[3], p1_recv.at[3], mate))
    for c in sd + p1:
        c.start()
    for c in [c_z, c_md, c_pair] + c_proj + [c_ci] + c_y + c_n:
        c.start()
    idrow_v[0] = jnp.full((8, 128), ids_s[0] * NC, I32)
    idcol_v[0] = idrow_v[0]

    ix = [rcopy(idrow_v.at[0], idrow_v.at[r], ix_send.at[r], ix_recv.at[r], row_dev(r)) for r in range(1, ROW)]
    iz = [
        rcopy(idcol_v.at[0], idcol_v.at[k], iz_send.at[k], iz_recv.at[k], sub_dev(ROW * k))
        for k in range(1, PLANES)
    ]
    for c in ix + iz:
        c.start()

    c_z.wait()
    zhi, zlo = split(z_v[...])
    lhs_v[0:COLS, :] = rbf_v[...]
    lhs_v[COLS : 2 * COLS, :] = (res_v[...] - rbf_v[...].astype(F32)).astype(BF16)
    lhs_v[2 * COLS : 2 * COLS + NC, :] = zhi
    lhs_v[2 * COLS + NC :, :] = zlo
    at_face = lax.broadcasted_iota(I32, (ROWS, FS), 0)
    for f in range(2):
        st_v[f] = one_hot(at_face == sdof_v[pl.ds(f, 1), :])
        zsf_v[f] = mm_nn(lhs_v[2 * COLS : 2 * COLS + NC, :], st_v[f]).astype(BF16)
    zs = [
        rcopy(zsf_v, zsin_v.at[o], zs_send.at[o], zs_recv.at[o], sub_dev(-REACH[o])) for o in range(4)
    ]
    for c in zs:
        c.start()

    c_pair.wait()
    lane = lax.broadcasted_iota(I32, (1, SUBS), 1)

    def entry(j, k):
        line = pair_v[j, pl.ds(k, 1), :].astype(F32)
        return jnp.sum(jnp.where(lane == s, line, 0.0), axis=1, keepdims=True).astype(I32)

    near = [(entry(j, 0) - s + (SUBS + 2)) & (SUBS - 1) for j in range(PAIRS)]
    face = [entry(j, 1) for j in range(PAIRS)]
    slot_e = [1 - core, 4 - core, 4 * core, 3 - 2 * core]
    for j in range(PAIRS):
        here = jnp.broadcast_to(near[j], (16, 128))
        side = jnp.broadcast_to(face[j], (16, 128))
        for q in range(4):
            hot = jnp.where(here == slot_e[q], 1.0, 0.0)
            w32_v[j, q] = hot[0:8]
            w16_v[j, q] = hot.astype(BF16)
            hot = jnp.where(here == REACH[q] + 2, 1.0, 0.0)
            v32_v[j, q] = hot[0:8]
            for k in range(2):
                v16_v[j, q, k] = jnp.where(side == k, hot, 0.0).astype(BF16)

    c_md.wait()

    def make_g(j, c):
        line = mdof_v[pl.ds(j, 1), :]
        gt_v[j] = one_hot(lax.broadcasted_iota(I32, (ROWS, FM), 0) == line)
        for lo in range(0, FM, 256):
            w = pl.ds(lo, 256)
            got = mm_nn(lhs_v[...], gt_v[j, :, w])
            rg_v[j, :, w] = got[0:COLS] + got[COLS : 2 * COLS]
            zg_v[j, :, w] = got[2 * COLS :].astype(BF16)
        return c

    lax.fori_loop(0, PAIRS, make_g, 0)
    res_part = mm_nt(lhs_v[2 * COLS :, :], rbf_v[...])
    part_v[...] = res_part[:NC] + res_part[NC:] + mm_nt(
        lhs_v[2 * COLS : 2 * COLS + NC, :], lhs_v[COLS : 2 * COLS, :]
    )

    for c in sd:
        c.wait_recv()
    for j in range(PAIRS):
        code = jnp.broadcast_to(near[j] * 2 + face[j], (1, FS))
        line = jnp.zeros((1, FS), I32)
        for o in range(4):
            for k in range(2):
                line = line + jnp.where(code == (REACH[o] + 2) * 2 + k, sdin_v[o, pl.ds(k, 1), :], 0)
        st_v[j] = one_hot(at_face == line)

    for c in ix + iz:
        c.wait()
    gap = lax.broadcasted_iota(I32, (NC, CBLK * NC), 1) - lax.broadcasted_iota(I32, (NC, CBLK * NC), 0)
    for k in range(PLANES):
        ecol_v[k * NC : (k + 1) * NC, :] = one_hot(gap == idcol_v[k][0:1, 0:1])
    for r in range(ROW):
        erow_v[r * NC : (r + 1) * NC, :] = one_hot(gap == idrow_v[(ROW - r) % ROW][0:1, 0:1])
    c_ci.wait()
    chi, clo = split(cinv_v[...])
    t1_v[0] = mm_nt(chi, ecol_v[...]).astype(BF16)
    t1_v[1] = mm_nt(clo, ecol_v[...]).astype(BF16)
    for k in range(2):
        a_v[k] = mm_nn(erow_v[...], t1_v[k]).astype(BF16)

    fw = [
        rcopy(half(rin_v.at[q], core), half(rin_v.at[q], core), fw_send.at[q], fw_recv.at[q], mate)
        for q in range(2)
    ]
    got = [
        rcopy(half(rbf_v, 0), half(rin_v.at[q], core), p1_send.at[0], p1_recv.at[q], mate) for q in range(2)
    ]
    for q in range(2):
        got[q].wait_recv()
        fw[q].start()
    for c in c_proj:
        c.wait()
    p1[2].wait_recv()
    p1[3].wait_recv()
    for q in range(2):
        fw[q].wait_recv()

    for j in range(PAIRS):
        there = rin_v[0] * jnp.tile(w16_v[j, 0], (8, 9))
        for q in range(1, 4):
            there = there + rin_v[q] * jnp.tile(w16_v[j, q], (8, 9))
        tr_v[j] = mm_nn(there, st_v[j]).astype(BF16)
    for j in range(PAIRS):
        mhi, mlo = split(mm_nn(tr_v[j], proj_v[j]) - rg_v[j])
        mm_v[j, 0:COLS, :] = mhi
        mm_v[j, COLS:, :] = mlo
        ret_v[j] = mm_nt(mhi, proj_v[j]).astype(BF16)

    swc, cdc, abc = [], [], []
    for ch in range(CHUNKS):
        swc.append(rcopy(ab_v.at[ch, 1 - core], sw_v.at[ch], sw_send.at[ch], sw_recv.at[ch], mate))
        cdc.append([
            rcopy(cd_v.at[ch, 0], rpin_v.at[1, ch], cd_send.at[ch, 0], cd_recv.at[ch, 0],
                  chip_dev(shared_step, core)),
            rcopy(cd_v.at[ch, 1], rpin_v.at[2, ch], cd_send.at[ch, 1], cd_recv.at[ch, 1], mate),
        ])
        abc.append([
            rcopy(sum_v.at[ch, q], half(rpin_v.at[0, ch], core), ab_send.at[ch, q], ab_recv.at[ch, core],
                  chip_dev(2 * q - 1, 1 - q))
            for q in range(2)
        ])

    def add_swapped(ch):
        swc[ch].wait_recv()
        for q in range(2):
            mine = ab32_v[ch, q, pl.ds(pl.multiple_of(core * HALF, HALF), HALF), :]
            sum_v[ch, q] = (mine + sw_v[ch, q].astype(F32)).astype(BF16)
            abc[ch][q].start()

    cc = [rcopy(c_v.at[o], cin_v.at[o], c_send.at[o], c_recv.at[o], sub_dev(REACH[o])) for o in range(4)]

    def own_share():
        part = jnp.zeros((2 * NC, 2 * COLS), F32)
        for j in range(PAIRS):
            part = part + mm_nt(zg_v[j], mm_v[j])
        part_v[...] += 0.5 * (part[:NC, :COLS] + part[NC:, :COLS] + part[:NC, COLS:])

    def share():
        for c in zs:
            c.wait_recv()
        shares = []
        for j in range(PAIRS):
            zsel = jnp.zeros((NC, FS), BF16)
            for o in range(4):
                for k in range(2):
                    zsel = zsel + zsin_v[o, k] * jnp.tile(v16_v[j, o, k], (3, 6))
            shares.append(mm_nt(zsel, ret_v[j]))
        for o in range(4):
            total = shares[0] * jnp.tile(v32_v[0, o], (6, 1))
            for j in range(1, PAIRS):
                total = total + shares[j] * jnp.tile(v32_v[j, o], (6, 1))
            c_v[o] = (-0.5 * total).astype(BF16)
            cc[o].start()

    for ch in range(CHUNKS):
        for j in range(PAIRS):
            t_v[j] = mm_nt(ret_v[j], st_v[j, pl.ds(ch * CW, CW), :])
        for q in range(4):
            total = t_v[0] * jnp.tile(w32_v[0, q], (16, 3))
            for j in range(1, PAIRS):
                total = total + t_v[j] * jnp.tile(w32_v[j, q], (16, 3))
            if q < 2:
                ab32_v[ch, q] = total
                for h in range(2):
                    ab_v[ch, h, q] = total[h * HALF : (h + 1) * HALF].astype(BF16)
            else:
                cd_v[ch, q - 2] = total.astype(BF16)
            if q == 1:
                swc[ch].start()
        cdc[ch][0].start()
        cdc[ch][1].start()
        if ch == 0:
            share()
            own_share()
        else:
            add_swapped(ch - 1)
    add_swapped(CHUNKS - 1)

    def scatter(ch):
        at = pl.ds(ch * CW, CW)
        moved = mm_nt(mm_v[0], gt_v[0, at, :])
        for j in range(1, PAIRS):
            moved = moved + mm_nt(mm_v[j], gt_v[j, at, :])
        base_v[:, at] = res_v[:, at] + 0.5 * (moved[:COLS] + moved[COLS:])

    part = part_v[...]
    for o in range(4):
        cc[o].wait_recv()
        part = part + cin_v[o].astype(F32)
    col_v[0] = part.astype(BF16)
    pz = [
        rcopy(col_v.at[0], col_v.at[k], pz_send.at[k], pz_recv.at[k], sub_dev(ROW * k))
        for k in range(1, PLANES)
    ]
    for c in pz:
        c.start()

    def gcopy(src, ch, slot, h, k, step):
        part_of = (pl.ds(h * HALF, HALF), pl.ds(ch * CW, CW))
        return rcopy(x_v.at[(src,) + part_of], x_v.at[(slot,) + part_of], g_send.at[ch, k], g_recv.at[ch, k], grp_dev(step))

    gat = []
    for ch in range(CHUNKS):
        gat.append([
            gcopy(0, ch, 1, 0, 0, 1),
            gcopy(0, ch, 2, 1, 1, 3),
            gcopy(0, ch, 1, 1, 2, 1),
            gcopy(0, ch, 2, 0, 3, 3),
            gcopy(1, ch, 3, 0, 4, 1),
            gcopy(2, ch, 3, 1, 5, 3),
        ])

    def balance(ch):
        at = pl.ds(ch * CW, CW)
        cdc[ch][0].wait_recv()
        cdc[ch][1].wait_recv()
        for h in range(2):
            rcopy(sum_v.at[ch, 0], half(rpin_v.at[0, ch], h), ab_send.at[ch, 0], ab_recv.at[ch, h], mate).wait_recv()
        back = rpin_v[0, ch].astype(F32) + rpin_v[1, ch].astype(F32) + rpin_v[2, ch].astype(F32)
        new = base_v[:, at] - 0.5 * back
        base_v[:, at] = new
        x_v[0, pl.ds(0, COLS), at] = new.astype(BF16)
        for k in range(4):
            gat[ch][k].start()

    def forward(ch):
        gat[ch][0].wait_recv()
        gat[ch][4].start()
        gat[ch][1].wait_recv()
        gat[ch][5].start()

    def solve(block):
        return mm_nt(neu_v[block], x_v[block])

    scatter(0)
    balance(0)
    scatter(1)
    balance(1)

    for c in pz:
        c.wait()
    column = col_v[...].reshape(PLANES * NC, COLS)
    made = (mm_nn(a_v[0], column) + mm_nn(a_v[1], column)).astype(BF16)
    for r in range(ROW):
        pxo_v[r] = made[r * NC : (r + 1) * NC]
    px = [rcopy(pxo_v.at[r], pxi_v.at[r], px_send.at[r], px_recv.at[r], row_dev(r)) for r in range(1, ROW)]
    for c in px:
        c.start()
    scatter(2)
    balance(2)
    c_bal = local(base_v, bal_h.at[0], 18)
    c_bal.start()
    forward(0)
    for c in c_y + c_n:
        c.wait()
    for r in range(GROUPS):
        x_v[r, pl.ds(COLS, NC), :] = y_v[r].astype(BF16)
    zt_v[...] = z_v[...].T

    accy_v[...] = mm_nt(neu_v[3], x_v[3, pl.ds(COLS, NC), :])
    forward(1)
    mine = pxo_v[0].astype(F32)
    for r in range(1, ROW):
        px[r - 1].wait()
        mine = mine + pxi_v[r].astype(F32)
    m_v[0] = mine
    mc = [rcopy(m_v.at[0], m_v.at[r], m_send.at[r], m_recv.at[r], grp_dev(r)) for r in range(1, 4)]
    for c in mc:
        c.start()
    acc_v[...] = solve(0)
    forward(2)
    for q in range(2):
        for ch in range(CHUNKS):
            gat[ch][2 + q].wait_recv()
        acc_v[...] += solve(1 + q)
    w_v[...] = (zt_v[...] - accy_v[...] - acc_v[:, pl.ds(COLS, NC)]).astype(BF16)
    for ch in range(CHUNKS - 1):
        gat[ch][4].wait_recv()
        gat[ch][5].wait_recv()
    early = pl.ds(0, (CHUNKS - 1) * CW)
    total = acc_v[:, 0:COLS] + mm_nt(neu_v[3, :, early], x_v[3, pl.ds(0, COLS), early])
    for c in mc:
        c.wait()
    mhi, mlo = split(m_v[0] + m_v[1] + m_v[2] + m_v[3])
    from_m = mm_nn(w_v[...], jnp.concatenate([mhi, mlo], 1))
    acc_v[:, 0:COLS] = total + from_m[:, :COLS] + from_m[:, COLS:]
    gat[CHUNKS - 1][4].wait_recv()
    gat[CHUNKS - 1][5].wait_recv()
    late = pl.ds((CHUNKS - 1) * CW, CW)
    total = acc_v[:, 0:COLS] + mm_nt(neu_v[3, :, late], x_v[3, pl.ds(0, COLS), late])
    cor_v[...] = total.T
    c_cor = local(cor_v, cor_h.at[0], 19)
    c_cor.start()
    for c in sd + zs + cc + p1 + fw + swc:
        c.wait_send()
    for ch in range(CHUNKS):
        for c in cdc[ch] + abc[ch] + gat[ch]:
            c.wait_send()
    c_bal.wait()
    c_cor.wait()


def hand_over(a_ref, b_ref, x_ref, y_ref):
    x_ref[...] = a_ref[...]
    y_ref[...] = b_ref[...]


def local_part(
    residual, neumann, projection, pair_list, slave_dofs, master_dofs, zbasis, ybasis, coarse_inverse, coarse_ids
):
    any_spec = pl.BlockSpec(memory_space=pl.ANY)
    smem_spec = pl.BlockSpec(memory_space=pltpu.SMEM)
    dma = pltpu.SemaphoreType.DMA
    vm = pltpu.VMEM
    region = jax.ShapeDtypeStruct((1, COLS, ROWS), F32)
    scratch = [
        vm((PAIRS, 2, SUBS), I32),
        vm((COLS, ROWS), F32),
        vm((COLS, ROWS), BF16),
        vm((2 * COLS + 2 * NC, ROWS), BF16),
        vm((4, COLS, ROWS), BF16),
        vm((2, FS), I32),
        vm((4, 2, FS), I32),
        vm((PAIRS, FM), I32),
        vm((PAIRS, FS, FM), BF16),
        vm((PAIRS, ROWS, FM), BF16),
        vm((PAIRS, COLS, FM), F32),
        vm((PAIRS, 2 * NC, FM), BF16),
        vm((PAIRS, ROWS, FS), BF16),
        vm((2, NC, FS), BF16),
        vm((4, 2, NC, FS), BF16),
        vm((GROUPS, ROWS, ROWS), BF16),
        vm((NC, ROWS), F32),
        vm((GROUPS, NC, ROWS), F32),
        vm((CBLK * NC, CBLK * NC), F32),
        vm((ROW, 8, 128), I32),
        vm((PLANES, 8, 128), I32),
        vm((PLANES * NC, CBLK * NC), BF16),
        vm((ROW * NC, CBLK * NC), BF16),
        vm((2, CBLK * NC, PLANES * NC), BF16),
        vm((2, ROW * NC, PLANES * NC), BF16),
        vm((4, NC, COLS), BF16),
        vm((4, NC, COLS), BF16),
        vm((PLANES, NC, COLS), BF16),
        vm((ROW, NC, COLS), BF16),
        vm((ROW, NC, COLS), BF16),
        vm((GROUPS, NC, COLS), F32),
        vm((ROWS, NC), BF16),
        vm((ROWS, NC), F32),
        vm((ROWS, NC), F32),
        vm((PAIRS, 4, 8, 128), F32),
        vm((PAIRS, 4, 16, 128), BF16),
        vm((PAIRS, 4, 8, 128), F32),
        vm((PAIRS, 4, 2, 16, 128), BF16),
        vm((COLS, ROWS), F32),
        vm((NC, COLS), F32),
        vm((PAIRS, COLS, FS), BF16),
        vm((PAIRS, 2 * COLS, FM), BF16),
        vm((PAIRS, COLS, FS), BF16),
        vm((PAIRS, COLS, CW), F32),
        vm((CHUNKS, 2, COLS, CW), F32),
        vm((CHUNKS, 2, 2, HALF, CW), BF16),
        vm((CHUNKS, 2, COLS, CW), BF16),
        vm((CHUNKS, 2, HALF, CW), BF16),
        vm((CHUNKS, 2, HALF, CW), BF16),
        vm((3, CHUNKS, COLS, CW), BF16),
        vm((GROUPS, COLS + NC, ROWS), BF16),
        vm((ROWS, COLS + NC), F32),
        vm((COLS, ROWS), F32),
        dma((20,)),
        dma((4,)), dma((4,)), dma((4,)), dma((4,)), dma((4,)), dma((4,)),
        dma((4,)), dma((4,)), dma((2,)), dma((2,)),
        dma((CHUNKS,)), dma((CHUNKS,)), dma((CHUNKS, 2)), dma((CHUNKS, 2)), dma((CHUNKS, 2)), dma((CHUNKS, 2)),
        dma((ROW,)), dma((ROW,)), dma((PLANES,)), dma((PLANES,)),
        dma((ROW,)), dma((ROW,)), dma((PLANES,)), dma((PLANES,)),
        dma((CHUNKS, 6)), dma((CHUNKS, 6)), dma((4,)), dma((4,)),
    ]
    outs = pl.pallas_call(
        kernel,
        out_shape=(region, region),
        in_specs=[any_spec, smem_spec] + [any_spec] * 8,
        out_specs=(any_spec, any_spec),
        scratch_shapes=scratch,
        compiler_params=pltpu.CompilerParams(
            collective_id=0, has_side_effects=True, vmem_limit_bytes=60 * 1024 * 1024
        ),
    )(
        jnp.transpose(pair_list, (1, 2, 3, 0)), coarse_ids, residual, neumann, projection,
        slave_dofs, master_dofs, zbasis, ybasis, coarse_inverse,
    )
    whole = pl.BlockSpec(memory_space=pltpu.VMEM)
    return pl.pallas_call(
        hand_over,
        out_shape=(region, region),
        in_specs=[whole, whole],
        out_specs=(whole, whole),
    )(*outs)


def solution(mesh):
    placed = (
        P("sub", None, "grp"),
        P("sub", "grp", None),
        P("sub", "grp", None, None, None),
        P(),
        P("sub", "grp", None, None),
        P("sub", "grp", None, None),
        P("sub", None, None),
        P("sub", None, None),
        P(),
        P("sub"),
    )
    return jax.shard_map(
        local_part,
        mesh=mesh,
        in_specs=placed,
        out_specs=(P("sub", None, "grp"), P("sub", None, "grp")),
        check_vma=False,
    )
```

```python
import jax
import jax.numpy as jnp
from jax import lax
from jax.experimental import pallas as pl
from jax.experimental.pallas import tpu as pltpu
from jax.sharding import PartitionSpec as P

FS = 768
FM = 1024
NC = 48
COLS = 128
PAIRS = 4
ROWS = 1152
SUBS = 32
GROUPS = 4
CBLK = 16
REACH = (-2, -1, 1, 2)
HALF = COLS // 2
CHUNKS = 3
CW = ROWS // CHUNKS
ROW = 8
PLANES = SUBS // ROW
CHIPS = SUBS // 2
F32 = jnp.float32
BF16 = jnp.bfloat16
I32 = jnp.int32
MESH = pl.DeviceIdType.MESH


def mm_nn(a, b):
    return lax.dot_general(a, b, (((1,), (0,)), ((), ())), preferred_element_type=F32)


def mm_nt(a, b):
    return lax.dot_general(a, b, (((1,), (1,)), ((), ())), preferred_element_type=F32)


def split(x):
    hi = x.astype(BF16)
    return hi, (x - hi.astype(F32)).astype(BF16)


def one_hot(cond):
    return jnp.where(cond, 1.0, 0.0).astype(BF16)


def kernel(
    pair_h, ids_s, res_h, neu_h, proj_h, sdof_h, mdof_h, zb_h, yb_h, cinv_h,
    bal_h, cor_h,
    pair_v, res_v, rbf_v, lhs_v, rin_v, sdof_v, sdin_v, mdof_v, proj_v, gt_v, rg_v, zg_v, st_v,
    zsf_v, zsin_v, neu_v, z_v, y_v, cinv_v, idrow_v, idcol_v, ecol_v, erow_v, t1_v, a_v,
    c_v, cin_v, col_v, pxo_v, pxi_v, m_v, w_v, zt_v, accy_v, w32_v, w16_v, v32_v, v16_v,
    base_v, part_v, tr_v, mm_v, ret_v, t_v, ab32_v, ab_v, cd_v, sw_v, sum_v, rpin_v, x_v, acc_v, cor_v,
    loc_sem, sd_send, sd_recv, zs_send, zs_recv, c_send, c_recv, p1_send, p1_recv, fw_send, fw_recv,
    sw_send, sw_recv, cd_send, cd_recv, ab_send, ab_recv,
    ix_send, ix_recv, iz_send, iz_recv, px_send, px_recv, pz_send, pz_recv,
    g_send, g_recv, m_send, m_recv,
):
    s = lax.axis_index("sub")
    g = lax.axis_index("grp")
    core = lax.rem(s, 2)
    chip = lax.div(s, 2)
    row = lax.rem(s, ROW)

    def sub_dev(step):
        return (lax.rem(s + step + SUBS, SUBS), g)

    def chip_dev(step, c):
        return (lax.rem(chip + step + CHIPS, CHIPS) * 2 + c, g)

    def row_dev(r):
        return (s - row + lax.rem(row + r, ROW), g)

    def grp_dev(step):
        return (s, lax.rem(g + step, GROUPS))

    mate = (s + 1 - 2 * core, g)

    def local(src, dst, k):
        return pltpu.make_async_copy(src, dst, loc_sem.at[k])

    c_res = local(res_h.at[0], res_v, 0)
    c_sd = local(sdof_h.at[0, 0], sdof_v, 1)
    c_res.start()
    c_sd.start()

    barrier = pltpu.get_barrier_semaphore()
    greeted = [row_dev(r) for r in range(1, ROW)]
    greeted += [sub_dev(ROW * k) for k in range(1, PLANES)] + [grp_dev(k) for k in range(1, GROUPS)]
    expected = len(greeted)
    for k in REACH:
        outside = (row + k < 0) if k < 0 else (row + k >= ROW)
        expected = expected + jnp.where(outside, 1, 0)

        @pl.when(outside)
        def _():
            pl.semaphore_signal(barrier, inc=1, device_id=sub_dev(k), device_id_type=MESH)

    for dev in greeted:
        pl.semaphore_signal(barrier, inc=1, device_id=dev, device_id_type=MESH)

    order = [lax.rem(g + r, GROUPS) for r in (0, 3, 1, 2)]
    cols = [pl.ds(pl.multiple_of(q * ROWS, 128), ROWS) for q in order]
    c_md = local(mdof_h.at[0, 0], mdof_v, 2)
    c_pair = local(pair_h.at[g], pair_v, 3)
    c_proj = [local(proj_h.at[0, 0, j], proj_v.at[j], 4 + j) for j in range(PAIRS)]
    c_z = local(zb_h.at[0, :, cols[0]], z_v, 8)
    c_ci = local(cinv_h, cinv_v, 9)
    c_y = [local(yb_h.at[0, :, cols[r]], y_v.at[r], 10 + r) for r in range(GROUPS)]
    c_n = [local(neu_h.at[0, :, cols[r]], neu_v.at[r], 14 + r) for r in range(GROUPS)]
    c_res.wait()
    rbf_v[...] = res_v[...].astype(BF16)
    c_sd.wait()

    pl.semaphore_wait(barrier, expected)

    def rcopy(src, dst, ss, rs, dev):
        return pltpu.make_async_remote_copy(
            src_ref=src, dst_ref=dst, send_sem=ss, recv_sem=rs, device_id=dev, device_id_type=MESH
        )

    def half(ref, h):
        return ref.at[pl.ds(pl.multiple_of(h * HALF, HALF), HALF)]

    sd = [
        rcopy(sdof_v, sdin_v.at[o], sd_send.at[o], sd_recv.at[o], sub_dev(-REACH[o]))
        for o in range(4)
    ]
    shared_step = 2 * core - 1
    p1 = [
        rcopy(half(rbf_v, h), half(rin_v.at[1 - core], h), p1_send.at[h], p1_recv.at[1 - core],
              chip_dev(shared_step, h))
        for h in range(2)
    ]
    p1.append(rcopy(rbf_v, rin_v.at[2], p1_send.at[2], p1_recv.at[2], chip_dev(-shared_step, core)))
    p1.append(rcopy(rbf_v, rin_v.at[3], p1_send.at[3], p1_recv.at[3], mate))
    for c in sd + p1:
        c.start()
    for c in [c_z, c_md, c_pair] + c_proj + [c_ci] + c_y + c_n:
        c.start()
    idrow_v[0] = jnp.full((8, 128), ids_s[0] * NC, I32)
    idcol_v[0] = idrow_v[0]

    ix = [rcopy(idrow_v.at[0], idrow_v.at[r], ix_send.at[r], ix_recv.at[r], row_dev(r)) for r in range(1, ROW)]
    iz = [
        rcopy(idcol_v.at[0], idcol_v.at[k], iz_send.at[k], iz_recv.at[k], sub_dev(ROW * k))
        for k in range(1, PLANES)
    ]
    for c in ix + iz:
        c.start()

    c_z.wait()
    zhi, zlo = split(z_v[...])
    lhs_v[0:COLS, :] = rbf_v[...]
    lhs_v[COLS : 2 * COLS, :] = (res_v[...] - rbf_v[...].astype(F32)).astype(BF16)
    lhs_v[2 * COLS : 2 * COLS + NC, :] = zhi
    lhs_v[2 * COLS + NC :, :] = zlo
    at_face = lax.broadcasted_iota(I32, (ROWS, FS), 0)
    for f in range(2):
        st_v[f] = one_hot(at_face == sdof_v[pl.ds(f, 1), :])
        zsf_v[f] = mm_nn(lhs_v[2 * COLS : 2 * COLS + NC, :], st_v[f]).astype(BF16)
    zs = [
        rcopy(zsf_v, zsin_v.at[o], zs_send.at[o], zs_recv.at[o], sub_dev(-REACH[o])) for o in range(4)
    ]
    for c in zs:
        c.start()

    c_pair.wait()
    lane = lax.broadcasted_iota(I32, (1, SUBS), 1)

    def entry(j, k):
        line = pair_v[j, pl.ds(k, 1), :].astype(F32)
        return jnp.sum(jnp.where(lane == s, line, 0.0), axis=1, keepdims=True).astype(I32)

    near = [(entry(j, 0) - s + (SUBS + 2)) & (SUBS - 1) for j in range(PAIRS)]
    face = [entry(j, 1) for j in range(PAIRS)]
    slot_e = [1 - core, 4 - core, 4 * core, 3 - 2 * core]
    for j in range(PAIRS):
        here = jnp.broadcast_to(near[j], (16, 128))
        side = jnp.broadcast_to(face[j], (16, 128))
        for q in range(4):
            hot = jnp.where(here == slot_e[q], 1.0, 0.0)
            w32_v[j, q] = hot[0:8]
            w16_v[j, q] = hot.astype(BF16)
            hot = jnp.where(here == REACH[q] + 2, 1.0, 0.0)
            v32_v[j, q] = hot[0:8]
            for k in range(2):
                v16_v[j, q, k] = jnp.where(side == k, hot, 0.0).astype(BF16)

    c_md.wait()

    def make_g(j, c):
        line = mdof_v[pl.ds(j, 1), :]
        gt_v[j] = one_hot(lax.broadcasted_iota(I32, (ROWS, FM), 0) == line)
        for lo in range(0, FM, 256):
            w = pl.ds(lo, 256)
            got = mm_nn(lhs_v[...], gt_v[j, :, w])
            rg_v[j, :, w] = got[0:COLS] + got[COLS : 2 * COLS]
            zg_v[j, :, w] = got[2 * COLS :].astype(BF16)
        return c

    lax.fori_loop(0, PAIRS, make_g, 0)
    res_part = mm_nt(lhs_v[2 * COLS :, :], rbf_v[...])
    part_v[...] = res_part[:NC] + res_part[NC:] + mm_nt(
        lhs_v[2 * COLS : 2 * COLS + NC, :], lhs_v[COLS : 2 * COLS, :]
    )

    for c in sd:
        c.wait_recv()
    for j in range(PAIRS):
        code = jnp.broadcast_to(near[j] * 2 + face[j], (1, FS))
        line = jnp.zeros((1, FS), I32)
        for o in range(4):
            for k in range(2):
                line = line + jnp.where(code == (REACH[o] + 2) * 2 + k, sdin_v[o, pl.ds(k, 1), :], 0)
        st_v[j] = one_hot(at_face == line)

    for c in ix + iz:
        c.wait()
    gap = lax.broadcasted_iota(I32, (NC, CBLK * NC), 1) - lax.broadcasted_iota(I32, (NC, CBLK * NC), 0)
    for k in range(PLANES):
        ecol_v[k * NC : (k + 1) * NC, :] = one_hot(gap == idcol_v[k][0:1, 0:1])
    for r in range(ROW):
        erow_v[r * NC : (r + 1) * NC, :] = one_hot(gap == idrow_v[(ROW - r) % ROW][0:1, 0:1])
    c_ci.wait()
    chi, clo = split(cinv_v[...])
    t1_v[0] = mm_nt(chi, ecol_v[...]).astype(BF16)
    t1_v[1] = mm_nt(clo, ecol_v[...]).astype(BF16)
    for k in range(2):
        a_v[k] = mm_nn(erow_v[...], t1_v[k]).astype(BF16)

    fw = [
        rcopy(half(rin_v.at[q], core), half(rin_v.at[q], core), fw_send.at[q], fw_recv.at[q], mate)
        for q in range(2)
    ]
    got = [
        rcopy(half(rbf_v, 0), half(rin_v.at[q], core), p1_send.at[0], p1_recv.at[q], mate) for q in range(2)
    ]
    for q in range(2):
        got[q].wait_recv()
        fw[q].start()
    for c in c_proj:
        c.wait()
    p1[2].wait_recv()
    p1[3].wait_recv()
    for q in range(2):
        fw[q].wait_recv()

    for j in range(PAIRS):
        there = rin_v[0] * jnp.tile(w16_v[j, 0], (8, 9))
        for q in range(1, 4):
            there = there + rin_v[q] * jnp.tile(w16_v[j, q], (8, 9))
        tr_v[j] = mm_nn(there, st_v[j]).astype(BF16)
    for j in range(PAIRS):
        mhi, mlo = split(mm_nn(tr_v[j], proj_v[j]) - rg_v[j])
        mm_v[j, 0:COLS, :] = mhi
        mm_v[j, COLS:, :] = mlo
        ret_v[j] = mm_nt(mhi, proj_v[j]).astype(BF16)

    swc, cdc, abc = [], [], []
    for ch in range(CHUNKS):
        swc.append(rcopy(ab_v.at[ch, 1 - core], sw_v.at[ch], sw_send.at[ch], sw_recv.at[ch], mate))
        cdc.append([
            rcopy(cd_v.at[ch, 0], rpin_v.at[1, ch], cd_send.at[ch, 0], cd_recv.at[ch, 0],
                  chip_dev(shared_step, core)),
            rcopy(cd_v.at[ch, 1], rpin_v.at[2, ch], cd_send.at[ch, 1], cd_recv.at[ch, 1], mate),
        ])
        abc.append([
            rcopy(sum_v.at[ch, q], half(rpin_v.at[0, ch], core), ab_send.at[ch, q], ab_recv.at[ch, core],
                  chip_dev(2 * q - 1, 1 - q))
            for q in range(2)
        ])

    def add_swapped(ch):
        swc[ch].wait_recv()
        for q in range(2):
            mine = ab32_v[ch, q, pl.ds(pl.multiple_of(core * HALF, HALF), HALF), :]
            sum_v[ch, q] = (mine + sw_v[ch, q].astype(F32)).astype(BF16)
            abc[ch][q].start()

    cc = [rcopy(c_v.at[o], cin_v.at[o], c_send.at[o], c_recv.at[o], sub_dev(REACH[o])) for o in range(4)]

    def own_share():
        part = jnp.zeros((2 * NC, 2 * COLS), F32)
        for j in range(PAIRS):
            part = part + mm_nt(zg_v[j], mm_v[j])
        part_v[...] += 0.5 * (part[:NC, :COLS] + part[NC:, :COLS] + part[:NC, COLS:])

    def share():
        for c in zs:
            c.wait_recv()
        shares = []
        for j in range(PAIRS):
            zsel = jnp.zeros((NC, FS), BF16)
            for o in range(4):
                for k in range(2):
                    zsel = zsel + zsin_v[o, k] * jnp.tile(v16_v[j, o, k], (3, 6))
            shares.append(mm_nt(zsel, ret_v[j]))
        for o in range(4):
            total = shares[0] * jnp.tile(v32_v[0, o], (6, 1))
            for j in range(1, PAIRS):
                total = total + shares[j] * jnp.tile(v32_v[j, o], (6, 1))
            c_v[o] = (-0.5 * total).astype(BF16)
            cc[o].start()

    for ch in range(CHUNKS):
        for j in range(PAIRS):
            t_v[j] = mm_nt(ret_v[j], st_v[j, pl.ds(ch * CW, CW), :])
        for q in range(4):
            total = t_v[0] * jnp.tile(w32_v[0, q], (16, 3))
            for j in range(1, PAIRS):
                total = total + t_v[j] * jnp.tile(w32_v[j, q], (16, 3))
            if q < 2:
                ab32_v[ch, q] = total
                for h in range(2):
                    ab_v[ch, h, q] = total[h * HALF : (h + 1) * HALF].astype(BF16)
            else:
                cd_v[ch, q - 2] = total.astype(BF16)
            if q == 1:
                swc[ch].start()
        cdc[ch][0].start()
        cdc[ch][1].start()
        if ch == 0:
            share()
            add_swapped(0)
            own_share()
        elif ch == 2:
            add_swapped(1)

    def scatter(ch):
        at = pl.ds(ch * CW, CW)
        moved = mm_nt(mm_v[0], gt_v[0, at, :])
        for j in range(1, PAIRS):
            moved = moved + mm_nt(mm_v[j], gt_v[j, at, :])
        base_v[:, at] = res_v[:, at] + 0.5 * (moved[:COLS] + moved[COLS:])

    scatter(0)
    add_swapped(CHUNKS - 1)

    def gcopy(src, ch, slot, h, k, step):
        part_of = (pl.ds(h * HALF, HALF), pl.ds(ch * CW, CW))
        return rcopy(x_v.at[(src,) + part_of], x_v.at[(slot,) + part_of], g_send.at[ch, k], g_recv.at[ch, k], grp_dev(step))

    gat = []
    for ch in range(CHUNKS):
        gat.append([
            gcopy(0, ch, 1, 0, 0, 1),
            gcopy(0, ch, 2, 1, 1, 3),
            gcopy(0, ch, 1, 1, 2, 1),
            gcopy(0, ch, 2, 0, 3, 3),
            gcopy(1, ch, 3, 0, 4, 1),
            gcopy(2, ch, 3, 1, 5, 3),
        ])

    def balance(ch):
        at = pl.ds(ch * CW, CW)
        cdc[ch][0].wait_recv()
        cdc[ch][1].wait_recv()
        for h in range(2):
            rcopy(sum_v.at[ch, 0], half(rpin_v.at[0, ch], h), ab_send.at[ch, 0], ab_recv.at[ch, h], mate).wait_recv()
        back = rpin_v[0, ch].astype(F32) + rpin_v[1, ch].astype(F32) + rpin_v[2, ch].astype(F32)
        new = base_v[:, at] - 0.5 * back
        base_v[:, at] = new
        x_v[0, pl.ds(0, COLS), at] = new.astype(BF16)
        for k in range(4):
            gat[ch][k].start()

    def forward(ch):
        gat[ch][0].wait_recv()
        gat[ch][4].start()
        gat[ch][1].wait_recv()
        gat[ch][5].start()

    def solve(block):
        return mm_nt(neu_v[block], x_v[block])

    balance(0)

    part = part_v[...]
    for o in range(4):
        cc[o].wait_recv()
        part = part + cin_v[o].astype(F32)
    col_v[0] = part.astype(BF16)
    pz = [
        rcopy(col_v.at[0], col_v.at[k], pz_send.at[k], pz_recv.at[k], sub_dev(ROW * k))
        for k in range(1, PLANES)
    ]
    for c in pz:
        c.start()
    scatter(1)
    balance(1)

    for c in pz:
        c.wait()
    column = col_v[...].reshape(PLANES * NC, COLS)
    made = (mm_nn(a_v[0], column) + mm_nn(a_v[1], column)).astype(BF16)
    for r in range(ROW):
        pxo_v[r] = made[r * NC : (r + 1) * NC]
    px = [rcopy(pxo_v.at[r], pxi_v.at[r], px_send.at[r], px_recv.at[r], row_dev(r)) for r in range(1, ROW)]
    for c in px:
        c.start()
    scatter(2)
    balance(2)
    c_bal = local(base_v, bal_h.at[0], 18)
    c_bal.start()
    forward(0)
    for c in c_y + c_n:
        c.wait()
    for r in range(GROUPS):
        x_v[r, pl.ds(COLS, NC), :] = y_v[r].astype(BF16)
    zt_v[...] = z_v[...].T

    accy_v[...] = mm_nt(neu_v[3], x_v[3, pl.ds(COLS, NC), :])
    forward(1)
    mine = pxo_v[0].astype(F32)
    for r in range(1, ROW):
        px[r - 1].wait()
        mine = mine + pxi_v[r].astype(F32)
    m_v[0] = mine
    mc = [rcopy(m_v.at[0], m_v.at[r], m_send.at[r], m_recv.at[r], grp_dev(r)) for r in range(1, 4)]
    for c in mc:
        c.start()
    acc_v[...] = solve(0)
    forward(2)
    for q in range(2):
        for ch in range(CHUNKS):
            gat[ch][2 + q].wait_recv()
        acc_v[...] += solve(1 + q)
    w_v[...] = (zt_v[...] - accy_v[...] - acc_v[:, pl.ds(COLS, NC)]).astype(BF16)
    for ch in range(CHUNKS - 1):
        gat[ch][4].wait_recv()
        gat[ch][5].wait_recv()
    early = pl.ds(0, (CHUNKS - 1) * CW)
    total = acc_v[:, 0:COLS] + mm_nt(neu_v[3, :, early], x_v[3, pl.ds(0, COLS), early])
    for c in mc:
        c.wait()
    mhi, mlo = split(m_v[0] + m_v[1] + m_v[2] + m_v[3])
    from_m = mm_nn(w_v[...], jnp.concatenate([mhi, mlo], 1))
    acc_v[:, 0:COLS] = total + from_m[:, :COLS] + from_m[:, COLS:]
    gat[CHUNKS - 1][4].wait_recv()
    gat[CHUNKS - 1][5].wait_recv()
    late = pl.ds((CHUNKS - 1) * CW, CW)
    total = acc_v[:, 0:COLS] + mm_nt(neu_v[3, :, late], x_v[3, pl.ds(0, COLS), late])
    cor_v[...] = total.T
    c_cor = local(cor_v, cor_h.at[0], 19)
    c_cor.start()
    for c in sd + zs + cc + p1 + fw + swc:
        c.wait_send()
    for ch in range(CHUNKS):
        for c in cdc[ch] + abc[ch] + gat[ch]:
            c.wait_send()
    c_bal.wait()
    c_cor.wait()


def hand_over(a_ref, b_ref, x_ref, y_ref):
    x_ref[...] = a_ref[...]
    y_ref[...] = b_ref[...]


def local_part(
    residual, neumann, projection, pair_list, slave_dofs, master_dofs, zbasis, ybasis, coarse_inverse, coarse_ids
):
    any_spec = pl.BlockSpec(memory_space=pl.ANY)
    smem_spec = pl.BlockSpec(memory_space=pltpu.SMEM)
    dma = pltpu.SemaphoreType.DMA
    vm = pltpu.VMEM
    region = jax.ShapeDtypeStruct((1, COLS, ROWS), F32)
    scratch = [
        vm((PAIRS, 2, SUBS), I32),
        vm((COLS, ROWS), F32),
        vm((COLS, ROWS), BF16),
        vm((2 * COLS + 2 * NC, ROWS), BF16),
        vm((4, COLS, ROWS), BF16),
        vm((2, FS), I32),
        vm((4, 2, FS), I32),
        vm((PAIRS, FM), I32),
        vm((PAIRS, FS, FM), BF16),
        vm((PAIRS, ROWS, FM), BF16),
        vm((PAIRS, COLS, FM), F32),
        vm((PAIRS, 2 * NC, FM), BF16),
        vm((PAIRS, ROWS, FS), BF16),
        vm((2, NC, FS), BF16),
        vm((4, 2, NC, FS), BF16),
        vm((GROUPS, ROWS, ROWS), BF16),
        vm((NC, ROWS), F32),
        vm((GROUPS, NC, ROWS), F32),
        vm((CBLK * NC, CBLK * NC), F32),
        vm((ROW, 8, 128), I32),
        vm((PLANES, 8, 128), I32),
        vm((PLANES * NC, CBLK * NC), BF16),
        vm((ROW * NC, CBLK * NC), BF16),
        vm((2, CBLK * NC, PLANES * NC), BF16),
        vm((2, ROW * NC, PLANES * NC), BF16),
        vm((4, NC, COLS), BF16),
        vm((4, NC, COLS), BF16),
        vm((PLANES, NC, COLS), BF16),
        vm((ROW, NC, COLS), BF16),
        vm((ROW, NC, COLS), BF16),
        vm((GROUPS, NC, COLS), F32),
        vm((ROWS, NC), BF16),
        vm((ROWS, NC), F32),
        vm((ROWS, NC), F32),
        vm((PAIRS, 4, 8, 128), F32),
        vm((PAIRS, 4, 16, 128), BF16),
        vm((PAIRS, 4, 8, 128), F32),
        vm((PAIRS, 4, 2, 16, 128), BF16),
        vm((COLS, ROWS), F32),
        vm((NC, COLS), F32),
        vm((PAIRS, COLS, FS), BF16),
        vm((PAIRS, 2 * COLS, FM), BF16),
        vm((PAIRS, COLS, FS), BF16),
        vm((PAIRS, COLS, CW), F32),
        vm((CHUNKS, 2, COLS, CW), F32),
        vm((CHUNKS, 2, 2, HALF, CW), BF16),
        vm((CHUNKS, 2, COLS, CW), BF16),
        vm((CHUNKS, 2, HALF, CW), BF16),
        vm((CHUNKS, 2, HALF, CW), BF16),
        vm((3, CHUNKS, COLS, CW), BF16),
        vm((GROUPS, COLS + NC, ROWS), BF16),
        vm((ROWS, COLS + NC), F32),
        vm((COLS, ROWS), F32),
        dma((20,)),
        dma((4,)), dma((4,)), dma((4,)), dma((4,)), dma((4,)), dma((4,)),
        dma((4,)), dma((4,)), dma((2,)), dma((2,)),
        dma((CHUNKS,)), dma((CHUNKS,)), dma((CHUNKS, 2)), dma((CHUNKS, 2)), dma((CHUNKS, 2)), dma((CHUNKS, 2)),
        dma((ROW,)), dma((ROW,)), dma((PLANES,)), dma((PLANES,)),
        dma((ROW,)), dma((ROW,)), dma((PLANES,)), dma((PLANES,)),
        dma((CHUNKS, 6)), dma((CHUNKS, 6)), dma((4,)), dma((4,)),
    ]
    outs = pl.pallas_call(
        kernel,
        out_shape=(region, region),
        in_specs=[any_spec, smem_spec] + [any_spec] * 8,
        out_specs=(any_spec, any_spec),
        scratch_shapes=scratch,
        compiler_params=pltpu.CompilerParams(
            collective_id=0, has_side_effects=True, vmem_limit_bytes=60 * 1024 * 1024
        ),
    )(
        jnp.transpose(pair_list, (1, 2, 3, 0)), coarse_ids, residual, neumann, projection,
        slave_dofs, master_dofs, zbasis, ybasis, coarse_inverse,
    )
    whole = pl.BlockSpec(memory_space=pltpu.VMEM)
    return pl.pallas_call(
        hand_over,
        out_shape=(region, region),
        in_specs=[whole, whole],
        out_specs=(whole, whole),
    )(*outs)


def solution(mesh):
    placed = (
        P("sub", None, "grp"),
        P("sub", "grp", None),
        P("sub", "grp", None, None, None),
        P(),
        P("sub", "grp", None, None),
        P("sub", "grp", None, None),
        P("sub", None, None),
        P("sub", None, None),
        P(),
        P("sub"),
    )
    return jax.shard_map(
        local_part,
        mesh=mesh,
        in_specs=placed,
        out_specs=(P("sub", None, "grp"), P("sub", None, "grp")),
        check_vma=False,
    )
```
